256 devices in a mesh: section: 4 (over y_lo, core), ctx: 64 (over y_hi, x, z).
Axes of the slice: x: 4, y: 4 (y_hi: 2, y_lo: 2; y = y_hi * 2 + y_lo), z: 8, core: 2. Of those that a mesh axis runs over, the one named last changes fastest.
Arguments:
- tokens: bfloat16 [2, 8192, 2048], P(None, 'ctx'), may hold values from -6 to 6
- qkv_weight: bfloat16 [4, 2048, 3072], P('section', 'ctx'), may hold values from -0.125 to 0.125
- out_weight: bfloat16 [4, 1024, 2048], P('section', 'ctx'), may hold values from -0.1875 to 0.1875
- log_decay: float32 [4, 2, 8192, 16], P('section', None, 'ctx'), may hold values from -1.5 to 0, as said below
Outputs:
- hidden_states: bfloat16 [4, 2, 8192, 2048], P('section', None, 'ctx')
The draws below stay inside these ranges and needn't reach their ends.
Inputs may be any that keep to these rules, and one draw needn't show every extreme that they name: `log_decay`: every value is negative.
All inputs are finite; a program needn't handle non-finite values.
Results may differ from the reference program's by a relative error of at most 0.025.
Values may be sent and summed in bfloat16 or wider, within the bound.
No kernel may reach another device: no remote copies, remote signals or barrier semaphores. Data moves between devices by JAX's collectives and lax.ppermute only.
A program may use at most 128 MiB of HBM per device.

```python
import jax
import jax.numpy as jnp
from jax import lax

D = 2048
MIXER_HEADS = 16
HEAD = 64
TOK_DEV = 128
MICRO_BATCHES = 2
LAYER_TOTAL = 4
SEQUENCE_LENGTH = 8192
N_CTX = 64


def draw_log_decay(key, part):
    key_rows_list = jax.random.split(key, 7)
    slow_share = 0.5
    head_shape = (LAYER_TOTAL, 1, 1, 1, MIXER_HEADS)
    slow_heads = jax.random.bernoulli(key_rows_list[0], slow_share, head_shape)
    fast_rate = jax.random.uniform(key_rows_list[1], head_shape, jnp.float32, 1.0 / 50.0, 1.0 / 30.0)
    slow_total = jax.random.uniform(key_rows_list[2], head_shape, jnp.float32, 0.1, 0.45)
    base_rate = jnp.where(slow_heads, slow_total / SEQUENCE_LENGTH, fast_rate)
    device_factor = jax.random.uniform(key_rows_list[3], (LAYER_TOTAL, MICRO_BATCHES, N_CTX, 1, MIXER_HEADS), jnp.float32, 0.6, 1.4)
    position_factor = jnp.clip(1.0 + 0.2 * jax.random.normal(key_rows_list[4], (LAYER_TOTAL, MICRO_BATCHES, N_CTX, TOK_DEV, MIXER_HEADS), jnp.float32), 0.6, 1.4)
    decay_rate = (base_rate * device_factor * position_factor).reshape(LAYER_TOTAL, MICRO_BATCHES, SEQUENCE_LENGTH, MIXER_HEADS)
    spurt_position_list = jax.random.randint(key_rows_list[5], (LAYER_TOTAL, MICRO_BATCHES, 2), 0, SEQUENCE_LENGTH)
    spurt_keep_mask = jax.random.uniform(key_rows_list[6], (LAYER_TOTAL, MICRO_BATCHES, 2, MIXER_HEADS), jnp.float32, 0.5, 0.8)
    position_index = jnp.arange(SEQUENCE_LENGTH, dtype=jnp.int32)
    match_count = (position_index[None, None, None, :] == spurt_position_list[:, :, :, None]).astype(jnp.float32)
    spurt_state_sum = jnp.einsum('kgay,kgae->kgye', match_count, jnp.log(spurt_keep_mask))
    return -decay_rate + spurt_state_sum


def block_levels(own_key, shape, cuts, least, largest):
    def one(dim, blocks):
        heights = jax.random.uniform(jax.random.fold_in(jax.random.fold_in(own_key, 6), dim), (blocks,), jnp.float32, least / len(cuts), largest / len(cuts))
        return jnp.repeat(jnp.exp(heights), shape[dim] // blocks).reshape((-1,) + (1,) * (len(shape) - dim - 1))

    gain = one(*cuts[0])
    for cut in cuts[1:]:
        gain = gain * one(*cut)
    return gain


def noise(rng, shape, spread, reach, pieces=(), kind=jnp.bfloat16):
    gain = block_levels(rng, shape, pieces, -0.22, 0.18) if pieces else 1.0
    entries = jax.random.normal(rng, shape, jnp.float32) * spread * gain
    return jnp.minimum(jnp.maximum(entries, -reach), reach).astype(kind)


def setup_inputs(seed: int = 0) -> dict:
    key_of = jax.random.split(jax.random.key(seed), 5)
    tokens = noise(key_of[0], (MICRO_BATCHES, SEQUENCE_LENGTH, D), 1.0, 6.0, ((1, 64),))
    qkv_weight = noise(key_of[1], (LAYER_TOTAL, D, 3 * MIXER_HEADS * HEAD), D ** -0.5, 0.125, ((0, 4), (1, 64)))
    out_weight = noise(key_of[2], (LAYER_TOTAL, MIXER_HEADS * HEAD, D), (MIXER_HEADS * HEAD) ** -0.5, 0.1875, ((0, 4), (1, 64)))
    log_decay = draw_log_decay(jax.random.fold_in(key_of[4], 71), 0)
    return {"tokens": tokens, "qkv_weight": qkv_weight, "out_weight": out_weight, "log_decay": log_decay}


def round_low(value_rows):
    return lax.optimization_barrier(value_rows.astype(jnp.bfloat16)).astype(jnp.float32)

def apply_layer(inputs, weight, out_proj, decay):
    seq_len, model_width = inputs.shape
    head_count = decay.shape[1]
    wide_input = inputs.astype(jnp.float32)
    normed = (wide_input * lax.rsqrt(lax.optimization_barrier(jnp.mean(wide_input * wide_input, axis=-1, keepdims=True)) + 1e-05)).astype(jnp.bfloat16)
    projected = jnp.dot(normed, weight, preferred_element_type=jnp.float32).astype(jnp.bfloat16)
    inner = projected.shape[1] // 3
    head_dim = inner // head_count
    blocks = seq_len // TOK_DEV
    query_rows = projected[:, :inner].reshape(blocks, TOK_DEV, head_count, head_dim).astype(jnp.float32)
    key_block = projected[:, inner:2 * inner].reshape(blocks, TOK_DEV, head_count, head_dim).astype(jnp.float32)
    value_rows = projected[:, 2 * inner:].reshape(blocks, TOK_DEV, head_count, head_dim).astype(jnp.float32)
    cumulative = jnp.cumsum(decay.reshape(blocks, TOK_DEV, head_count), axis=1)
    ending = cumulative[:, -1]
    key_rows_scaled = round_low(key_block * jnp.exp(ending[:, None, :] - cumulative)[..., None])
    block_state = jnp.einsum('bjhk,bjhv->bhkv', key_rows_scaled, value_rows)
    totals = jnp.exp(ending)

    def carry_step(carried, block_item):
        block_total, state_here = block_item
        return (block_total[:, None, None] * carried + state_here, carried)
    start = jnp.zeros((head_count, head_dim, head_dim), jnp.float32)
    _, carried = lax.scan(carry_step, start, (totals, block_state))
    carried_state_low = round_low(carried)
    scores = jnp.einsum('bthk,bjhk->bhtj', query_rows, key_block)
    per_head = jnp.transpose(cumulative, (0, 2, 1))
    decay_gap = per_head[:, :, :, None] - per_head[:, :, None, :]
    position_index = jnp.arange(TOK_DEV, dtype=jnp.int32)
    causal = position_index[:, None] >= position_index[None, :]
    weights = round_low(jnp.where(causal, scores * jnp.exp(jnp.where(causal, decay_gap, 0.0)), 0.0))
    intra_out = jnp.einsum('bhtj,bjhv->bthv', weights, value_rows)
    inter_out = jnp.einsum('bthk,bhkv->bthv', query_rows, carried_state_low) * jnp.exp(cumulative)[..., None]
    mixture = intra_out + inter_out
    normed_out = mixture * lax.rsqrt(lax.optimization_barrier(jnp.mean(mixture * mixture, axis=-1, keepdims=True)) + 1e-05)
    mixed_low = normed_out.reshape(seq_len, inner).astype(jnp.bfloat16)
    mixed = jnp.dot(mixed_low, out_proj, preferred_element_type=jnp.float32)
    return (wide_input + mixed).astype(jnp.bfloat16)

def reference(tokens, qkv_weight, out_weight, log_decay):
    layer_outputs = []
    current = [tokens[micro_index] for micro_index in range(MICRO_BATCHES)]
    for layer_index in range(LAYER_TOTAL):
        current = [apply_layer(current[micro_index], qkv_weight[layer_index], out_weight[layer_index], log_decay[layer_index, micro_index]) for micro_index in range(MICRO_BATCHES)]
        layer_outputs.append(jnp.stack(current, axis=0))
    return jnp.stack(layer_outputs, axis=0)
```

```python
import functools

import jax
import jax.numpy as jnp
from jax import lax
from jax.experimental import pallas as pl
from jax.experimental.pallas import tpu as pltpu
from jax.sharding import Mesh, PartitionSpec as P

CTX = ("yhi", "x", "z")
SPREAD = ("core", "x", "z")
NB = 512
EPS = 1e-05


def swap(value, axis):
    return lax.ppermute(value, axis, [(0, 1), (1, 0)])


def half_mask(rows, lanes, half):
    return lax.broadcasted_iota(jnp.int32, (rows, lanes), 1) < half


def by_head(low, table, p):
    return jnp.where(low, table[:, 2 * p : 2 * p + 1], table[:, 2 * p + 1 : 2 * p + 2])


def project_kernel(x_ref, w_ref, scale_ref, proj_ref, state_ref, normed_ref):
    n = pl.program_id(0)
    rows, width = x_ref.shape
    half = width // 2
    inner = proj_ref.shape[1] // 3
    part = w_ref.shape[2] // 2

    @pl.when(n == 0)
    def _():
        x = x_ref[...].astype(jnp.float32)
        scale = lax.rsqrt(jnp.mean(x * x, axis=-1, keepdims=True) + EPS)
        normed_ref[...] = (x * scale).astype(jnp.bfloat16)

    acc = jnp.dot(
        normed_ref[:, :half],
        w_ref[0, :, :part, :].reshape(half, NB),
        preferred_element_type=jnp.float32,
    )
    acc += jnp.dot(
        normed_ref[:, half:],
        w_ref[0, :, part:, :].reshape(half, NB),
        preferred_element_type=jnp.float32,
    )
    proj_ref[:, pl.ds(pl.multiple_of(n * NB, NB), NB)] = acc.astype(jnp.bfloat16)

    @pl.when(n == pl.num_programs(0) - 1)
    def _():
        low = half_mask(rows, 128, 64)
        scale = scale_ref[...]
        for p in range(inner // 128):
            keys = proj_ref[:, inner + 128 * p : inner + 128 * (p + 1)].astype(jnp.float32)
            values = proj_ref[:, 2 * inner + 128 * p : 2 * inner + 128 * (p + 1)]
            scaled = (keys * by_head(low, scale, p)).astype(jnp.bfloat16)
            outer = lax.dot_general(
                scaled, values, (((0,), (0,)), ((), ())), preferred_element_type=jnp.float32
            )
            state_ref[64 * p : 64 * (p + 1), :] = jnp.where(
                low[:64], outer[:64], outer[64:]
            ).astype(jnp.bfloat16)


def project(x, weights, scale):
    rows, width = x.shape
    groups = weights.shape[1]
    share = width // groups
    inner = 1024
    blocks = 3 * inner // NB
    per_core = blocks // 2
    return pl.pallas_call(
        project_kernel,
        grid=(blocks,),
        in_specs=[
            pl.BlockSpec((rows, width), lambda n: (0, 0)),
            pl.BlockSpec((1, groups, share, NB), lambda n: (n // per_core, 0, n % per_core, 0)),
            pl.BlockSpec(scale.shape, lambda n: (0, 0)),
        ],
        out_specs=[
            pl.BlockSpec((rows, 3 * inner), lambda n: (0, 0)),
            pl.BlockSpec((inner // 2, 128), lambda n: (0, 0)),
        ],
        out_shape=[
            jax.ShapeDtypeStruct((rows, 3 * inner), jnp.bfloat16),
            jax.ShapeDtypeStruct((inner // 2, 128), jnp.bfloat16),
        ],
        scratch_shapes=[pltpu.VMEM((rows, width), jnp.bfloat16)],
        compiler_params=pltpu.CompilerParams(vmem_limit_bytes=24 * 2**20),
        cost_estimate=pl.CostEstimate(
            flops=2 * rows * width * 3 * inner, bytes_accessed=6 * width * inner, transcendentals=0
        ),
        name="project",
    )(x, weights, scale)


def within_kernel(proj_ref, cum_ref, cum_t_ref, out_ref):
    rows = proj_ref.shape[0]
    inner = proj_ref.shape[1] // 3
    low = half_mask(rows, 128, 64)
    causal = lax.broadcasted_iota(jnp.int32, (rows, rows), 0) >= lax.broadcasted_iota(
        jnp.int32, (rows, rows), 1
    )
    cum = cum_ref[...]
    cum_t = cum_t_ref[...]
    zero = jnp.zeros((rows, 128), jnp.bfloat16)
    for p in range(inner // 128):
        queries = proj_ref[:, 128 * p : 128 * (p + 1)]
        keys = proj_ref[:, inner + 128 * p : inner + 128 * (p + 1)]
        values = proj_ref[:, 2 * inner + 128 * p : 2 * inner + 128 * (p + 1)]
        weights = []
        for k in range(2):
            h = 2 * p + k
            own = jnp.where(low, queries, zero) if k == 0 else jnp.where(low, zero, queries)
            scores = lax.dot_general(
                own, keys, (((1,), (1,)), ((), ())), preferred_element_type=jnp.float32
            )
            gap = cum[:, h : h + 1] - cum_t[h : h + 1, :]
            decay = jnp.exp(jnp.where(causal, gap, 0.0))
            weights.append(jnp.where(causal, scores * decay, 0.0).astype(jnp.bfloat16))
        both = jnp.concatenate(
            [jnp.where(low, values, zero), jnp.where(low, zero, values)], axis=0
        )
        out_ref[:, 128 * p : 128 * (p + 1)] = jnp.dot(
            jnp.concatenate(weights, axis=1), both, preferred_element_type=jnp.float32
        )


def within(proj, cum, cum_t):
    rows, cols = proj.shape
    return pl.pallas_call(
        within_kernel,
        out_shape=jax.ShapeDtypeStruct((rows, cols // 3), jnp.float32),
        compiler_params=pltpu.CompilerParams(vmem_limit_bytes=16 * 2**20),
        cost_estimate=pl.CostEstimate(
            flops=2 * rows * rows * cols, bytes_accessed=4 * rows * cols, transcendentals=16 * rows * rows
        ),
        name="within",
    )(proj, cum, cum_t)


def carry_kernel(state_ref, total_ref, out_ref):
    carried = jnp.zeros(state_ref.shape[1:], jnp.float32)
    for c in range(state_ref.shape[0]):
        out_ref[c] = carried.astype(jnp.bfloat16)
        carried = total_ref[c : c + 1, :] * carried + state_ref[c].astype(jnp.float32)


def carry(states, totals):
    return pl.pallas_call(
        carry_kernel,
        out_shape=jax.ShapeDtypeStruct(states.shape, jnp.bfloat16),
        cost_estimate=pl.CostEstimate(flops=2 * states.size, bytes_accessed=4 * states.size, transcendentals=0),
        name="carry",
    )(states, totals)


def output_kernel(q_ref, carried_ref, grow_ref, within_ref, x_ref, w_ref, out_ref, mixed_ref):
    n = pl.program_id(0)
    rows, inner = within_ref.shape
    half = inner // 2
    part = w_ref.shape[2] // 2

    @pl.when(n == 0)
    def _():
        low = half_mask(rows, 128, 64)
        low64 = low[:64]
        zero = jnp.zeros((64, 128), jnp.bfloat16)
        grow = grow_ref[...]
        for p in range(inner // 128):
            cols = slice(128 * p, 128 * (p + 1))
            state = carried_ref[64 * p : 64 * (p + 1), :]
            both = jnp.concatenate(
                [jnp.where(low64, state, zero), jnp.where(low64, zero, state)], axis=0
            )
            earlier = jnp.dot(q_ref[:, cols], both, preferred_element_type=jnp.float32)
            mixture = within_ref[:, cols] + earlier * by_head(low, grow, p)
            square = mixture * mixture
            first = jnp.sum(jnp.where(low, square, 0.0), axis=-1, keepdims=True)
            second = jnp.sum(jnp.where(low, 0.0, square), axis=-1, keepdims=True)
            scale = jnp.where(
                low, lax.rsqrt(first * (1.0 / 64.0) + EPS), lax.rsqrt(second * (1.0 / 64.0) + EPS)
            )
            mixed_ref[:, cols] = (mixture * scale).astype(jnp.bfloat16)

    acc = jnp.dot(
        mixed_ref[:, :half],
        w_ref[0, :, :part, :].reshape(half, NB),
        preferred_element_type=jnp.float32,
    )
    acc += jnp.dot(
        mixed_ref[:, half:],
        w_ref[0, :, part:, :].reshape(half, NB),
        preferred_element_type=jnp.float32,
    )
    out_ref[...] = (x_ref[...].astype(jnp.float32) + acc).astype(jnp.bfloat16)


def output(proj, carried, grow, inside, x, weights):
    rows, width = x.shape
    inner = inside.shape[1]
    groups = weights.shape[1]
    share = inner // groups
    blocks = width // NB
    per_core = blocks // 2
    first = 3 * inner // 2 // NB * (width // groups) // share
    return pl.pallas_call(
        output_kernel,
        grid=(blocks,),
        in_specs=[
            pl.BlockSpec((rows, inner), lambda n: (0, 0)),
            pl.BlockSpec(carried.shape, lambda n: (0, 0)),
            pl.BlockSpec(grow.shape, lambda n: (0, 0)),
            pl.BlockSpec((rows, inner), lambda n: (0, 0)),
            pl.BlockSpec((rows, NB), lambda n: (0, n)),
            pl.BlockSpec(
                (1, groups, share, NB), lambda n: (n // per_core, 0, first + n % per_core, 0)
            ),
        ],
        out_specs=pl.BlockSpec((rows, NB), lambda n: (0, n)),
        out_shape=jax.ShapeDtypeStruct((rows, width), jnp.bfloat16),
        scratch_shapes=[pltpu.VMEM((rows, inner), jnp.bfloat16)],
        compiler_params=pltpu.CompilerParams(vmem_limit_bytes=24 * 2**20),
        cost_estimate=pl.CostEstimate(
            flops=2 * rows * width * inner, bytes_accessed=2 * width * inner, transcendentals=0
        ),
        name="output",
    )(proj, carried, grow, inside, x, weights)


def in_blocks(value):
    rows, cols = value.shape[-2:]
    split = value.reshape(value.shape[:-1] + (cols // NB, NB))
    return jnp.moveaxis(split, -2, -3)


def shared_weights(qkv, out, core):
    def halves(value):
        cols = value.shape[1] // 2
        low, high = value[:, :cols], value[:, cols:]
        keep = jnp.where(core == 0, low, high)
        other = swap(jnp.where(core == 0, high, low), "core")
        layers = jnp.stack([jnp.where(core == 0, keep, other), jnp.where(core == 0, other, keep)])
        return in_blocks(layers)

    parts = [halves(qkv), halves(out)]
    place = lax.axis_index("yhi")
    flat = []
    for part in parts:
        far = swap(part, "yhi")
        pair = jnp.stack(
            [jnp.where(place == 0, part, far), jnp.where(place == 0, far, part)], axis=2
        )
        flat.append(pair.reshape(2, -1, NB))
    own = jnp.concatenate(flat, axis=1)
    return [
        lax.all_gather(own[k], SPREAD, axis=0).reshape(2, -1, own.shape[1], NB) for k in range(2)
    ]


def decays(log_decay, core):
    keep = jnp.where(core == 0, log_decay[0], log_decay[1])
    other = swap(jnp.where(core == 0, log_decay[1], log_decay[0]), "core")
    both = [jnp.where(core == 0, keep, other), jnp.where(core == 0, other, keep)]
    rows, heads = keep.shape
    lower = jnp.tril(jnp.ones((rows, rows), jnp.float32))
    blocks = lax.axis_size(CTX)
    per_pair = blocks // (heads // 2)
    out, rows_sent = [], []
    for d in both:
        cum = jnp.dot(lower, d, precision=lax.Precision.HIGHEST)
        ending = cum[-1:]
        total = jnp.exp(ending[0])
        lanes = jnp.repeat(total.reshape(heads // 2, 2), 64, axis=1)
        rows_sent.append(jnp.repeat(lanes, per_pair, axis=0))
        out.append([cum, cum.T, jnp.exp(ending - cum), jnp.exp(cum)])
    sent = jnp.stack(rows_sent + [jnp.zeros_like(rows_sent[0])] * 6, axis=1)
    received = lax.all_to_all(sent, CTX, 0, 0, tiled=True)
    for k in range(2):
        out[k].append(received[:, k, :])
    return out


def shards(tokens, qkv_weight, out_weight, log_decay):
    core = lax.axis_index("core")
    level = lax.axis_index("ylo")
    blocks = lax.axis_size(CTX)
    x = lax.dynamic_index_in_dim(tokens, core, 0, False)
    weights = shared_weights(qkv_weight[0], out_weight[0], core)
    tables = decays(log_decay[0], core)
    kept = []
    for step in range(4):
        cum, cum_t, scale, grow, totals = tables[step % 2]
        w = weights[step % 2]
        if step == 2:
            x = lax.ppermute(x, "ylo", [(0, 1)])
        proj, state = project(x, w, scale)
        slices = lax.all_to_all(state.reshape(blocks, -1, 128), CTX, 0, 0, tiled=True)
        inside = within(proj, cum, cum_t)
        mine = carry(slices, totals)
        carried = lax.all_to_all(mine, CTX, 0, 0, tiled=True).reshape(state.shape)
        x = output(proj, carried, grow, inside, x, w)
        kept.append(x)
    first = jnp.where(level == 0, kept[0], kept[2])
    second = jnp.where(level == 0, kept[1], kept[3])
    other = swap(jnp.where(core == 0, second, first), "core")
    result = jnp.stack([jnp.where(core == 0, first, other), jnp.where(core == 0, other, second)])
    return result[None]


def solution(mesh):
    fine = Mesh(mesh.devices.reshape(2, 2, 2, 4, 8), ("ylo", "core") + CTX)
    section = ("ylo", "core")
    in_specs = (
        P(None, CTX, None),
        P(section, CTX, None),
        P(section, CTX, None),
        P(section, None, CTX, None),
    )
    return jax.shard_map(
        shards, mesh=fine, in_specs=in_specs, out_specs=P(section, None, CTX, None), check_vma=False
    )
```

```python
import functools

import jax
import jax.numpy as jnp
from jax import lax
from jax.experimental import pallas as pl
from jax.experimental.pallas import tpu as pltpu
from jax.sharding import Mesh, PartitionSpec as P

CTX = ("yhi", "x", "z")
SPREAD = ("core", "x", "z")
NB = 512
EPS = 1e-05
VMEM_KEPT = 36 * 2**20


def swap(value, axis):
    return lax.ppermute(value, axis, [(0, 1), (1, 0)])


def half_mask(rows, lanes, half):
    return lax.broadcasted_iota(jnp.int32, (rows, lanes), 1) < half


def by_head(low, table, p):
    return jnp.where(low, table[:, 2 * p : 2 * p + 1], table[:, 2 * p + 1 : 2 * p + 2])


def share_copies(blocks, layer, w_ref, buffer, sems):
    copies = []
    for k, (parts, rows) in enumerate(blocks):
        block, at = [], 0
        for i, (first, column, count) in enumerate(parts):
            for far in range(2):
                block.append(
                    pltpu.make_async_copy(
                        w_ref.at[layer, :, pl.ds(first + far * rows, rows), pl.ds(column, count)],
                        buffer.at[k, far, :, :, pl.ds(at, count)],
                        sems.at[k, 2 * i + far],
                    )
                )
            at += count
        copies.append(block)
    return copies


def start_all(copies):
    for block in copies:
        for copy in block:
            copy.start()


def block_dot(left, copies, buffer, k):
    for copy in copies[k]:
        copy.wait()
    return jnp.dot(left, buffer[k].reshape(left.shape[1], NB), preferred_element_type=jnp.float32)


def keys_kernel(blocks, layer, x_ref, w_ref, table_ref, kv_ref, state_ref, normed_ref, buffer, sems):
    copies = share_copies(blocks, layer, w_ref, buffer, sems)
    start_all(copies)
    rows = x_ref.shape[0]
    inner = kv_ref.shape[1] // 2
    x = x_ref[...].astype(jnp.float32)
    normed = (x * lax.rsqrt(jnp.mean(x * x, axis=-1, keepdims=True) + EPS)).astype(jnp.bfloat16)
    normed_ref[...] = normed
    low = half_mask(rows, 128, 64)
    scale = table_ref[:rows, 16:32]
    half = NB // 2
    for k in range(len(blocks)):
        part = block_dot(normed, copies, buffer, k).astype(jnp.bfloat16)
        kv_ref[:, half * k : half * (k + 1)] = part[:, :half]
        kv_ref[:, inner + half * k : inner + half * (k + 1)] = part[:, half:]
        for c in range(half // 128):
            p = half * k // 128 + c
            keys = part[:, 128 * c : 128 * (c + 1)].astype(jnp.float32) * by_head(low, scale, p)
            outer = lax.dot_general(
                keys.astype(jnp.bfloat16),
                part[:, half + 128 * c : half + 128 * (c + 1)],
                (((0,), (0,)), ((), ())),
                preferred_element_type=jnp.float32,
            )
            state_ref[64 * p : 64 * (p + 1), :] = jnp.where(
                low[:64], outer[:64], outer[64:]
            ).astype(jnp.bfloat16)


def project_keys(x, weights, layer, table):
    rows, width = x.shape
    inner = 1024
    share, half = width // 64, NB // 2
    row = 2 * share
    blocks = [
        ([(row * (2 + g // 2), half * (g % 2), half), (row * (4 + g // 2), half * (g % 2), half)], share)
        for g in range(4)
    ]
    vmem = pl.BlockSpec(memory_space=pltpu.VMEM)
    return pl.pallas_call(
        functools.partial(keys_kernel, blocks, layer),
        in_specs=[vmem, pl.BlockSpec(memory_space=pl.ANY), vmem],
        out_specs=[vmem] * 3,
        out_shape=[
            jax.ShapeDtypeStruct((rows, 2 * inner), jnp.bfloat16),
            jax.ShapeDtypeStruct((inner // 2, 128), jnp.bfloat16),
            jax.ShapeDtypeStruct((rows, width), jnp.bfloat16),
        ],
        scratch_shapes=[
            pltpu.VMEM((len(blocks), 2, 32, share, NB), jnp.bfloat16),
            pltpu.SemaphoreType.DMA((len(blocks), 4)),
        ],
        compiler_params=pltpu.CompilerParams(vmem_limit_bytes=VMEM_KEPT),
        cost_estimate=pl.CostEstimate(
            flops=4 * rows * width * inner, bytes_accessed=4 * width * inner, transcendentals=0
        ),
        name="keys",
    )(x, weights, table)


def within_kernel(blocks, layer, normed_ref, w_ref, kv_ref, table_ref, q_ref, out_ref, buffer, sems):
    copies = share_copies(blocks, layer, w_ref, buffer, sems)
    start_all(copies)
    rows = kv_ref.shape[0]
    inner = kv_ref.shape[1] // 2
    low = half_mask(rows, 128, 64)
    causal = lax.broadcasted_iota(jnp.int32, (rows, rows), 0) >= lax.broadcasted_iota(
        jnp.int32, (rows, rows), 1
    )
    cum = table_ref[:rows, :16]
    cum_t = table_ref[rows:, :]
    zero = jnp.zeros((rows, 128), jnp.bfloat16)
    normed = normed_ref[...]
    for p in range(inner // 128):
        if p % (NB // 128) == 0:
            k = 128 * p // NB
            part = block_dot(normed, copies, buffer, k).astype(jnp.bfloat16)
            q_ref[:, NB * k : NB * (k + 1)] = part
        at = 128 * p % NB
        queries = part[:, at : at + 128]
        keys = kv_ref[:, 128 * p : 128 * (p + 1)]
        values = kv_ref[:, inner + 128 * p : inner + 128 * (p + 1)]
        weights = []
        for k in range(2):
            h = 2 * p + k
            own = jnp.where(low, queries, zero) if k == 0 else jnp.where(low, zero, queries)
            scores = lax.dot_general(
                own, keys, (((1,), (1,)), ((), ())), preferred_element_type=jnp.float32
            )
            gap = cum[:, h : h + 1] - cum_t[h : h + 1, :]
            decay = jnp.exp(jnp.where(causal, gap, 0.0))
            weights.append(jnp.where(causal, scores * decay, 0.0).astype(jnp.bfloat16))
        both = jnp.concatenate(
            [jnp.where(low, values, zero), jnp.where(low, zero, values)], axis=0
        )
        out_ref[:, 128 * p : 128 * (p + 1)] = jnp.dot(
            jnp.concatenate(weights, axis=1), both, preferred_element_type=jnp.float32
        )


def within(normed, weights, layer, kv, table):
    rows, width = normed.shape
    inner = kv.shape[1] // 2
    share = width // 64
    blocks = [([(2 * share * n, 0, NB)], share) for n in range(2)]
    vmem = pl.BlockSpec(memory_space=pltpu.VMEM)
    return pl.pallas_call(
        functools.partial(within_kernel, blocks, layer),
        in_specs=[vmem, pl.BlockSpec(memory_space=pl.ANY), vmem, vmem],
        out_specs=[vmem] * 2,
        out_shape=[
            jax.ShapeDtypeStruct((rows, inner), jnp.bfloat16),
            jax.ShapeDtypeStruct((rows, inner), jnp.float32),
        ],
        scratch_shapes=[
            pltpu.VMEM((len(blocks), 2, 32, share, NB), jnp.bfloat16),
            pltpu.SemaphoreType.DMA((len(blocks), 2)),
        ],
        compiler_params=pltpu.CompilerParams(vmem_limit_bytes=VMEM_KEPT),
        cost_estimate=pl.CostEstimate(
            flops=2 * rows * width * inner + 6 * rows * rows * inner,
            bytes_accessed=2 * width * inner + 16 * rows * inner,
            transcendentals=16 * rows * rows,
        ),
        name="within",
    )(normed, weights, kv, table)


def carry_kernel(layer, state_ref, total_ref, out_ref):
    carried = jnp.zeros(state_ref.shape[1:], jnp.float32)
    for c in range(state_ref.shape[0]):
        out_ref[c] = carried.astype(jnp.bfloat16)
        carried = total_ref[c, layer : layer + 1, :] * carried + state_ref[c].astype(jnp.float32)


def carry(states, totals, layer):
    return pl.pallas_call(
        functools.partial(carry_kernel, layer),
        out_shape=jax.ShapeDtypeStruct(states.shape, jnp.bfloat16),
        compiler_params=pltpu.CompilerParams(vmem_limit_bytes=4 * 2**20),
        cost_estimate=pl.CostEstimate(
            flops=2 * states.size, bytes_accessed=4 * states.size, transcendentals=0
        ),
        name="carry",
    )(states, totals)


def output_kernel(
    blocks, layer, q_ref, carried_ref, table_ref, within_ref, x_ref, w_ref, out_ref, buffer, sems
):
    copies = share_copies(blocks, layer, w_ref, buffer, sems)
    start_all(copies)
    rows, inner = within_ref.shape
    low = half_mask(rows, 128, 64)
    low64 = low[:64]
    zero = jnp.zeros((64, 128), jnp.bfloat16)
    grow = table_ref[:rows, 32:48]
    mixed = []
    for p in range(inner // 128):
        cols = slice(128 * p, 128 * (p + 1))
        state = carried_ref[64 * p : 64 * (p + 1), :]
        both = jnp.concatenate(
            [jnp.where(low64, state, zero), jnp.where(low64, zero, state)], axis=0
        )
        earlier = jnp.dot(q_ref[:, cols], both, preferred_element_type=jnp.float32)
        mixture = within_ref[:, cols] + earlier * by_head(low, grow, p)
        square = mixture * mixture
        first = jnp.sum(jnp.where(low, square, 0.0), axis=-1, keepdims=True)
        second = jnp.sum(jnp.where(low, 0.0, square), axis=-1, keepdims=True)
        scale = jnp.where(
            low, lax.rsqrt(first * (1.0 / 64.0) + EPS), lax.rsqrt(second * (1.0 / 64.0) + EPS)
        )
        mixed.append((mixture * scale).astype(jnp.bfloat16))
    mixed = jnp.concatenate(mixed, axis=1)
    for k in range(len(blocks)):
        cols = slice(NB * k, NB * (k + 1))
        acc = block_dot(mixed, copies, buffer, k)
        out_ref[:, cols] = (x_ref[:, cols].astype(jnp.float32) + acc).astype(jnp.bfloat16)


def output(q, carried, table, inside, x, weights, layer):
    rows, width = x.shape
    inner = inside.shape[1]
    share = inner // 64
    first = 3 * inner // NB * (width // 64) * 2
    blocks = [([(first + 2 * share * n, 0, NB)], share) for n in range(4)]
    vmem = pl.BlockSpec(memory_space=pltpu.VMEM)
    return pl.pallas_call(
        functools.partial(output_kernel, blocks, layer),
        in_specs=[vmem] * 5 + [pl.BlockSpec(memory_space=pl.ANY)],
        out_specs=vmem,
        out_shape=jax.ShapeDtypeStruct((rows, width), jnp.bfloat16),
        scratch_shapes=[
            pltpu.VMEM((len(blocks), 2, 32, share, NB), jnp.bfloat16),
            pltpu.SemaphoreType.DMA((len(blocks), 2)),
        ],
        compiler_params=pltpu.CompilerParams(vmem_limit_bytes=VMEM_KEPT),
        cost_estimate=pl.CostEstimate(
            flops=2 * rows * width * inner, bytes_accessed=2 * width * inner, transcendentals=0
        ),
        name="output",
    )(q, carried, table, inside, x, weights)


def in_blocks(value):
    rows, cols = value.shape
    return jnp.moveaxis(value.reshape(rows, cols // NB, NB), 1, 0)


def shared_weights(qkv, out):
    place = lax.axis_index("yhi")
    flat = []
    for part in (in_blocks(qkv), in_blocks(out)):
        far = swap(part, "yhi")
        pair = [jnp.where(place == 0, part, far), jnp.where(place == 0, far, part)]
        flat.append(jnp.stack(pair, axis=1).reshape(-1, NB))
    own = jnp.concatenate(flat, axis=0)
    gathered = lax.all_gather(own, SPREAD, axis=0)
    return gathered.reshape(2, -1, own.shape[0], NB)


def decays(log_decay, core):
    keep = jnp.where(core == 0, log_decay[0], log_decay[1])
    other = swap(jnp.where(core == 0, log_decay[1], log_decay[0]), "core")
    both = [jnp.where(core == 0, keep, other), jnp.where(core == 0, other, keep)]
    rows, heads = keep.shape
    lower = jnp.tril(jnp.ones((rows, rows), jnp.float32))
    blocks = lax.axis_size(CTX)
    per_pair = blocks // (heads // 2)
    tables, rows_sent = [], []
    for d in both:
        cum = jnp.dot(lower, d, precision=lax.Precision.HIGHEST)
        ending = cum[-1:]
        total = jnp.exp(ending[0])
        lanes = jnp.repeat(total.reshape(heads // 2, 2), 64, axis=1)
        rows_sent.append(jnp.repeat(lanes, per_pair, axis=0))
        wide = jnp.concatenate([cum, jnp.exp(ending - cum), jnp.exp(cum)], axis=1)
        wide = jnp.pad(wide, ((0, 0), (0, rows - wide.shape[1])))
        tables.append(jnp.concatenate([wide, cum.T], axis=0))
    sent = jnp.stack(rows_sent + [jnp.zeros_like(rows_sent[0])] * 6, axis=1)
    return tables, lax.all_to_all(sent, CTX, 0, 0, tiled=True)


def shards(tokens, qkv_weight, out_weight, log_decay):
    core = lax.axis_index("core")
    level = lax.axis_index("ylo")
    blocks = lax.axis_size(CTX)
    x = lax.dynamic_index_in_dim(tokens, core, 0, False)
    weights = shared_weights(qkv_weight[0], out_weight[0])
    tables, totals = decays(log_decay[0], core)
    x, totals, tables = lax.optimization_barrier((x, totals, tables))
    kept = []
    for step in range(4):
        layer = step % 2
        table = tables[layer]
        if step == 2:
            x = lax.ppermute(x, "ylo", [(0, 1)])
        kv, state, normed = project_keys(x, weights, layer, table)
        slices = lax.all_to_all(state.reshape(blocks, -1, 128), CTX, 0, 0, tiled=True)
        q, inside = within(normed, weights, layer, kv, table)
        slices, inside = lax.optimization_barrier((slices, inside))
        mine = carry(slices, totals, layer)
        carried = lax.all_to_all(mine, CTX, 0, 0, tiled=True).reshape(state.shape)
        x = output(q, carried, table, inside, x, weights, layer)
        kept.append(x)
    first = jnp.where(level == 0, kept[0], kept[2])
    second = jnp.where(level == 0, kept[1], kept[3])
    other = swap(jnp.where(core == 0, second, first), "core")
    result = jnp.stack([jnp.where(core == 0, first, other), jnp.where(core == 0, other, second)])
    return result[None]


def solution(mesh):
    fine = Mesh(mesh.devices.reshape(2, 2, 2, 4, 8), ("ylo", "core") + CTX)
    section = ("ylo", "core")
    in_specs = (
        P(None, CTX, None),
        P(section, CTX, None),
        P(section, CTX, None),
        P(section, None, CTX, None),
    )
    return jax.shard_map(
        shards, mesh=fine, in_specs=in_specs, out_specs=P(section, None, CTX, None), check_vma=False
    )
```

```python
import functools

import jax
import jax.numpy as jnp
from jax import lax
from jax.experimental import pallas as pl
from jax.experimental.pallas import tpu as pltpu
from jax.sharding import Mesh, PartitionSpec as P

CTX = ("yhi", "x", "z")
SPREAD = ("core", "x", "z")
NB = 512
EPS = 1e-05
VMEM_KEPT = 50 * 2**20


def swap(value, axis):
    return lax.ppermute(value, axis, [(0, 1), (1, 0)])


def half_mask(rows, lanes, half):
    return lax.broadcasted_iota(jnp.int32, (rows, lanes), 1) < half


def by_head(low, table, p):
    return jnp.where(low, table[:, 2 * p : 2 * p + 1], table[:, 2 * p + 1 : 2 * p + 2])


def share_copies(blocks, w_ref, buffer, sems):
    copies = []
    stride = w_ref.shape[2] // 2
    for k, (rows, parts) in enumerate(blocks):
        block, at = [], 0
        for side, first, column, count in parts:
            for far in range(2):
                source = w_ref.at[side, :, pl.ds(far * stride + first, rows), pl.ds(column, count)]
                goal = buffer.at[k, far, :, :, pl.ds(at, count)]
                block.append(pltpu.make_async_copy(source, goal, sems.at[k, len(block)]))
            at += count
        copies.append(block)
    return copies


def start_all(copies):
    for block in copies:
        for copy in block:
            copy.start()


def block_dot(left, copies, buffer, k):
    for copy in copies[k]:
        copy.wait()
    return jnp.dot(left, buffer[k].reshape(left.shape[1], NB), preferred_element_type=jnp.float32)


def normalized(x_ref):
    x = x_ref[...].astype(jnp.float32)
    return (x * lax.rsqrt(jnp.mean(x * x, axis=-1, keepdims=True) + EPS)).astype(jnp.bfloat16)


def keys_kernel(blocks, x_ref, w_ref, table_ref, kv_ref, state_ref, buffer, sems):
    copies = share_copies(blocks, w_ref, buffer, sems)
    start_all(copies)
    rows = x_ref.shape[0]
    inner = kv_ref.shape[1] // 2
    normed = normalized(x_ref)
    low = half_mask(rows, 128, 64)
    scale = table_ref[:rows, 16:32]
    half = NB // 2
    for k in range(len(blocks)):
        part = block_dot(normed, copies, buffer, k).astype(jnp.bfloat16)
        kv_ref[:, half * k : half * (k + 1)] = part[:, :half]
        kv_ref[:, inner + half * k : inner + half * (k + 1)] = part[:, half:]
        for c in range(half // 128):
            p = half * k // 128 + c
            keys = part[:, 128 * c : 128 * (c + 1)].astype(jnp.float32) * by_head(low, scale, p)
            outer = lax.dot_general(
                keys.astype(jnp.bfloat16),
                part[:, half + 128 * c : half + 128 * (c + 1)],
                (((0,), (0,)), ((), ())),
                preferred_element_type=jnp.float32,
            )
            state_ref[64 * p : 64 * (p + 1), :] = jnp.where(
                low[:64], outer[:64], outer[64:]
            ).astype(jnp.bfloat16)


def project_keys(x, weights, table):
    rows, width = x.shape
    inner = 1024
    share = width // 64
    half = NB // 2
    blocks = [
        (share, [(side, share * part, half * i, half) for part in (1, 2)])
        for side in range(2)
        for i in range(2)
    ]
    vmem = pl.BlockSpec(memory_space=pltpu.VMEM)
    return pl.pallas_call(
        functools.partial(keys_kernel, blocks),
        in_specs=[vmem, pl.BlockSpec(memory_space=pl.ANY), vmem],
        out_specs=[vmem] * 2,
        out_shape=[
            jax.ShapeDtypeStruct((rows, 2 * inner), jnp.bfloat16),
            jax.ShapeDtypeStruct((inner // 2, 128), jnp.bfloat16),
        ],
        scratch_shapes=[
            pltpu.VMEM((len(blocks), 2, 32, share, NB), jnp.bfloat16),
            pltpu.SemaphoreType.DMA((len(blocks), 4)),
        ],
        compiler_params=pltpu.CompilerParams(vmem_limit_bytes=VMEM_KEPT),
        cost_estimate=pl.CostEstimate(
            flops=4 * rows * width * inner, bytes_accessed=4 * width * inner, transcendentals=0
        ),
        name="keys",
    )(x, weights, table)


def within_kernel(blocks, x_ref, w_ref, kv_ref, table_ref, q_ref, out_ref, buffer, sems):
    copies = share_copies(blocks, w_ref, buffer, sems)
    start_all(copies)
    rows = kv_ref.shape[0]
    inner = kv_ref.shape[1] // 2
    low = half_mask(rows, 128, 64)
    causal = lax.broadcasted_iota(jnp.int32, (rows, rows), 0) >= lax.broadcasted_iota(
        jnp.int32, (rows, rows), 1
    )
    cum = table_ref[:rows, :16]
    cum_t = table_ref[rows:, :]
    zero = jnp.zeros((rows, 128), jnp.bfloat16)
    normed = normalized(x_ref)
    for p in range(inner // 128):
        if p % (NB // 128) == 0:
            k = 128 * p // NB
            part = block_dot(normed, copies, buffer, k).astype(jnp.bfloat16)
            q_ref[:, NB * k : NB * (k + 1)] = part
        at = 128 * p % NB
        queries = part[:, at : at + 128]
        keys = kv_ref[:, 128 * p : 128 * (p + 1)]
        values = kv_ref[:, inner + 128 * p : inner + 128 * (p + 1)]
        weights = []
        for k in range(2):
            h = 2 * p + k
            own = jnp.where(low, queries, zero) if k == 0 else jnp.where(low, zero, queries)
            scores = lax.dot_general(
                own, keys, (((1,), (1,)), ((), ())), preferred_element_type=jnp.float32
            )
            gap = cum[:, h : h + 1] - cum_t[h : h + 1, :]
            decay = jnp.exp(jnp.where(causal, gap, 0.0))
            weights.append(jnp.where(causal, scores * decay, 0.0).astype(jnp.bfloat16))
        both = jnp.concatenate(
            [jnp.where(low, values, zero), jnp.where(low, zero, values)], axis=0
        )
        out_ref[:, 128 * p : 128 * (p + 1)] = jnp.dot(
            jnp.concatenate(weights, axis=1), both, preferred_element_type=jnp.float32
        )


def within(x, weights, kv, table):
    rows, width = x.shape
    inner = kv.shape[1] // 2
    share = width // 64
    blocks = [(share, [(side, 0, 0, NB)]) for side in range(2)]
    vmem = pl.BlockSpec(memory_space=pltpu.VMEM)
    return pl.pallas_call(
        functools.partial(within_kernel, blocks),
        in_specs=[vmem, pl.BlockSpec(memory_space=pl.ANY), vmem, vmem],
        out_specs=[vmem] * 2,
        out_shape=[
            jax.ShapeDtypeStruct((rows, inner), jnp.bfloat16),
            jax.ShapeDtypeStruct((rows, inner), jnp.float32),
        ],
        scratch_shapes=[
            pltpu.VMEM((len(blocks), 2, 32, share, NB), jnp.bfloat16),
            pltpu.SemaphoreType.DMA((len(blocks), 2)),
        ],
        compiler_params=pltpu.CompilerParams(vmem_limit_bytes=VMEM_KEPT),
        cost_estimate=pl.CostEstimate(
            flops=2 * rows * width * inner + 6 * rows * rows * inner,
            bytes_accessed=2 * width * inner + 16 * rows * inner,
            transcendentals=16 * rows * rows,
        ),
        name="within",
    )(x, weights, kv, table)


def carry_kernel(state_ref, total_ref, out_ref):
    carried = jnp.zeros(state_ref.shape[1:], jnp.float32)
    for c in range(state_ref.shape[0]):
        out_ref[c] = carried.astype(jnp.bfloat16)
        carried = total_ref[c : c + 1, :] * carried + state_ref[c].astype(jnp.float32)


def carry(states, totals):
    return pl.pallas_call(
        carry_kernel,
        out_shape=jax.ShapeDtypeStruct(states.shape, jnp.bfloat16),
        compiler_params=pltpu.CompilerParams(vmem_limit_bytes=4 * 2**20),
        cost_estimate=pl.CostEstimate(
            flops=2 * states.size, bytes_accessed=4 * states.size, transcendentals=0
        ),
        name="carry",
    )(states, totals)


def output_kernel(
    blocks, q_ref, carried_ref, table_ref, within_ref, x_ref, w_ref, out_ref, buffer, sems
):
    copies = share_copies(blocks, w_ref, buffer, sems)
    start_all(copies)
    rows, inner = within_ref.shape
    low = half_mask(rows, 128, 64)
    low64 = low[:64]
    zero = jnp.zeros((64, 128), jnp.bfloat16)
    grow = table_ref[:rows, 32:48]
    mixed = []
    for p in range(inner // 128):
        cols = slice(128 * p, 128 * (p + 1))
        state = carried_ref[64 * p : 64 * (p + 1), :]
        both = jnp.concatenate(
            [jnp.where(low64, state, zero), jnp.where(low64, zero, state)], axis=0
        )
        earlier = jnp.dot(q_ref[:, cols], both, preferred_element_type=jnp.float32)
        mixture = within_ref[:, cols] + earlier * by_head(low, grow, p)
        square = mixture * mixture
        first = jnp.sum(jnp.where(low, square, 0.0), axis=-1, keepdims=True)
        second = jnp.sum(jnp.where(low, 0.0, square), axis=-1, keepdims=True)
        scale = jnp.where(
            low, lax.rsqrt(first * (1.0 / 64.0) + EPS), lax.rsqrt(second * (1.0 / 64.0) + EPS)
        )
        mixed.append((mixture * scale).astype(jnp.bfloat16))
    mixed = jnp.concatenate(mixed, axis=1)
    for k in range(len(blocks)):
        cols = slice(NB * k, NB * (k + 1))
        acc = block_dot(mixed, copies, buffer, k)
        out_ref[:, cols] = (x_ref[:, cols].astype(jnp.float32) + acc).astype(jnp.bfloat16)


def output(q, carried, table, inside, x, weights):
    rows, width = x.shape
    inner = inside.shape[1]
    share = inner // 64
    first = 3 * (width // 64)
    blocks = [(share, [(n // 2, first + share * (n % 2), 0, NB)]) for n in range(4)]
    vmem = pl.BlockSpec(memory_space=pltpu.VMEM)
    return pl.pallas_call(
        functools.partial(output_kernel, blocks),
        in_specs=[vmem] * 5 + [pl.BlockSpec(memory_space=pl.ANY)],
        out_specs=vmem,
        out_shape=jax.ShapeDtypeStruct((rows, width), jnp.bfloat16),
        scratch_shapes=[
            pltpu.VMEM((len(blocks), 2, 32, share, NB), jnp.bfloat16),
            pltpu.SemaphoreType.DMA((len(blocks), 2)),
        ],
        compiler_params=pltpu.CompilerParams(vmem_limit_bytes=VMEM_KEPT),
        cost_estimate=pl.CostEstimate(
            flops=2 * rows * width * inner, bytes_accessed=2 * width * inner, transcendentals=0
        ),
        name="output",
    )(q, carried, table, inside, x, weights)


def paired(low, high, core):
    keep = jnp.where(core == 0, low, high)
    other = swap(jnp.where(core == 0, high, low), "core")
    return jnp.where(core == 0, keep, other), jnp.where(core == 0, other, keep)


def across(value, axes):
    flip = [(0, 3), (1, 2), (2, 1), (3, 0)] if len(axes) == 2 else [(0, 1), (1, 0)]
    return lax.ppermute(value, axes, flip)


def shared_weights(qkv, out, core, level):
    rows, depth = qkv.shape[0], out.shape[0]
    inner = qkv.shape[1] // 3
    halves = []
    for side in range(2):
        cut = [qkv[:, inner * i + NB * side : inner * i + NB * (side + 1)] for i in range(3)]
        first = out.shape[1] // 2 * side
        cut += [out[:, first + NB * i : first + NB * (i + 1)] for i in range(2)]
        halves.append(jnp.concatenate(cut, axis=0))
    first, second = paired(halves[0], halves[1], core)
    stay = jnp.where(level == 0, first, second)
    leave = jnp.where(level == 0, second, first)
    far = across(stay, ("yhi",))
    come, come_far = across(leave, ("ylo",)), across(leave, ("ylo", "yhi"))
    place = lax.axis_index("yhi")
    gathered = []
    for layer in range(2):
        staying = level == layer
        pair = jnp.where(staying, stay, come), jnp.where(staying, far, come_far)
        own = jnp.concatenate(
            [jnp.where(place == 0, pair[0], pair[1]), jnp.where(place == 0, pair[1], pair[0])], axis=0
        )
        gathered.append(lax.all_gather(own, SPREAD, axis=0).reshape(2, -1, own.shape[0], NB))
    return gathered


def decays(log_decay, core, level):
    first, second = paired(log_decay[0], log_decay[1], core)
    come = across(jnp.where(level == 0, second, first), ("ylo",))
    both = [jnp.where(level == 0, first, come), jnp.where(level == 0, come, second)]
    rows, heads = first.shape
    lower = jnp.tril(jnp.ones((rows, rows), jnp.float32))
    blocks = lax.axis_size(CTX)
    per_pair = blocks // (heads // 2)
    tables, rows_sent = [], []
    for d in both:
        cum = jnp.dot(lower, d, precision=lax.Precision.HIGHEST)
        ending = cum[-1:]
        total = jnp.exp(ending[0])
        lanes = jnp.repeat(total.reshape(heads // 2, 2), 64, axis=1)
        rows_sent.append(jnp.repeat(lanes, per_pair, axis=0))
        wide = jnp.concatenate([cum, jnp.exp(ending - cum), jnp.exp(cum)], axis=1)
        wide = jnp.pad(wide, ((0, 0), (0, rows - wide.shape[1])))
        tables.append(jnp.concatenate([wide, cum.T], axis=0))
    sent = jnp.stack(rows_sent + [jnp.zeros_like(rows_sent[0])] * 6, axis=1)
    received = lax.all_to_all(sent, CTX, 0, 0, tiled=True)
    return tables, [received[:, k, :] for k in range(2)]


def shards(tokens, qkv_weight, out_weight, log_decay):
    core = lax.axis_index("core")
    level = lax.axis_index("ylo")
    blocks = lax.axis_size(CTX)
    x = lax.dynamic_index_in_dim(tokens, core, 0, False)
    weights = shared_weights(qkv_weight[0], out_weight[0], core, level)
    tables, totals = decays(log_decay[0], core, level)
    x, totals, tables = lax.optimization_barrier((x, totals, tables))
    kept = []
    for step in range(4):
        layer = step // 2
        table, w = tables[layer], weights[layer]
        if step > 0:
            x = lax.ppermute(x, "ylo", [(1 - step % 2, step % 2)])
            kept.append(x)
        kv, state = project_keys(x, w, table)
        slices = lax.all_to_all(state.reshape(blocks, -1, 128), CTX, 0, 0, tiled=True)
        q, inside = within(x, w, kv, table)
        slices, inside = lax.optimization_barrier((slices, inside))
        mine = carry(slices, totals[layer])
        carried = lax.all_to_all(mine, CTX, 0, 0, tiled=True).reshape(state.shape)
        x = output(q, carried, table, inside, x, w)
        kept.append(x)
    first = jnp.where(level == 0, kept[0], kept[5])
    second = jnp.where(level == 0, kept[3], kept[6])
    other = swap(jnp.where(core == 0, second, first), "core")
    result = jnp.stack([jnp.where(core == 0, first, other), jnp.where(core == 0, other, second)])
    return result[None]


def solution(mesh):
    fine = Mesh(mesh.devices.reshape(2, 2, 2, 4, 8), ("ylo", "core") + CTX)
    section = ("ylo", "core")
    in_specs = (
        P(None, CTX, None),
        P(section, CTX, None),
        P(section, CTX, None),
        P(section, None, CTX, None),
    )
    return jax.shard_map(
        shards, mesh=fine, in_specs=in_specs, out_specs=P(section, None, CTX, None), check_vma=False
    )
```

```python
import functools

import jax
import jax.numpy as jnp
from jax import lax
from jax.experimental import pallas as pl
from jax.experimental.pallas import tpu as pltpu
from jax.sharding import Mesh, PartitionSpec as P

CTX = ("yhi", "x", "z")
SPREAD = ("core", "x", "z")
NB = 512
EPS = 1e-05
VMEM_KEPT = 50 * 2**20


def swap(value, axis):
    return lax.ppermute(value, axis, [(0, 1), (1, 0)])


def half_mask(rows, lanes, half):
    return lax.broadcasted_iota(jnp.int32, (rows, lanes), 1) < half


def by_head(low, table, p):
    return jnp.where(low, table[:, 2 * p : 2 * p + 1], table[:, 2 * p + 1 : 2 * p + 2])


def share_copies(blocks, w_ref, buffer, sems):
    copies = []
    stride = w_ref.shape[2] // 2
    for k, (rows, parts) in enumerate(blocks):
        block, at = [], 0
        for side, first, column, count in parts:
            for far in range(2):
                source = w_ref.at[side, :, pl.ds(far * stride + first, rows), pl.ds(column, count)]
                goal = buffer.at[k, far, :, :, pl.ds(at, count)]
                block.append(pltpu.make_async_copy(source, goal, sems.at[k, len(block)]))
            at += count
        copies.append(block)
    return copies


def start_all(copies):
    for block in copies:
        for copy in block:
            copy.start()


def block_dot(left, copies, buffer, k):
    for copy in copies[k]:
        copy.wait()
    return jnp.dot(left, buffer[k].reshape(left.shape[1], NB), preferred_element_type=jnp.float32)


def normalized(x_ref):
    x = x_ref[...].astype(jnp.float32)
    return (x * lax.rsqrt(jnp.mean(x * x, axis=-1, keepdims=True) + EPS)).astype(jnp.bfloat16)


def keys_kernel(blocks, x_ref, w_ref, table_ref, kv_ref, state_ref, buffer, sems):
    copies = share_copies(blocks, w_ref, buffer, sems)
    start_all(copies)
    rows = x_ref.shape[0]
    inner = kv_ref.shape[1] // 2
    normed = normalized(x_ref)
    low = half_mask(rows, 128, 64)
    scale = table_ref[:rows, 16:32]
    half = NB // 2
    for k in range(len(blocks)):
        part = block_dot(normed, copies, buffer, k).astype(jnp.bfloat16)
        kv_ref[:, half * k : half * (k + 1)] = part[:, :half]
        kv_ref[:, inner + half * k : inner + half * (k + 1)] = part[:, half:]
        for c in range(half // 128):
            p = half * k // 128 + c
            keys = part[:, 128 * c : 128 * (c + 1)].astype(jnp.float32) * by_head(low, scale, p)
            outer = lax.dot_general(
                keys.astype(jnp.bfloat16),
                part[:, half + 128 * c : half + 128 * (c + 1)],
                (((0,), (0,)), ((), ())),
                preferred_element_type=jnp.float32,
            )
            state_ref[64 * p : 64 * (p + 1), :] = jnp.where(
                low[:64], outer[:64], outer[64:]
            ).astype(jnp.bfloat16)


def project_keys(x, weights, table):
    rows, width = x.shape
    inner = 1024
    share = width // 64
    half = NB // 2
    blocks = [
        (share, [(side, share * part, half * i, half) for part in (1, 2)])
        for side in range(2)
        for i in range(2)
    ]
    vmem = pl.BlockSpec(memory_space=pltpu.VMEM)
    return pl.pallas_call(
        functools.partial(keys_kernel, blocks),
        in_specs=[vmem, pl.BlockSpec(memory_space=pl.ANY), vmem],
        out_specs=[vmem] * 2,
        out_shape=[
            jax.ShapeDtypeStruct((rows, 2 * inner), jnp.bfloat16),
            jax.ShapeDtypeStruct((inner // 2, 128), jnp.bfloat16),
        ],
        scratch_shapes=[
            pltpu.VMEM((len(blocks), 2, 32, share, NB), jnp.bfloat16),
            pltpu.SemaphoreType.DMA((len(blocks), 4)),
        ],
        compiler_params=pltpu.CompilerParams(vmem_limit_bytes=VMEM_KEPT),
        cost_estimate=pl.CostEstimate(
            flops=4 * rows * width * inner, bytes_accessed=4 * width * inner, transcendentals=0
        ),
        name="keys",
    )(x, weights, table)


def within_kernel(blocks, x_ref, w_ref, kv_ref, table_ref, q_ref, out_ref, buffer, sems):
    copies = share_copies(blocks, w_ref, buffer, sems)
    start_all(copies)
    rows = kv_ref.shape[0]
    inner = kv_ref.shape[1] // 2
    low = half_mask(rows, 128, 64)
    causal = lax.broadcasted_iota(jnp.int32, (rows, rows), 0) >= lax.broadcasted_iota(
        jnp.int32, (rows, rows), 1
    )
    cum = table_ref[:rows, :16]
    cum_t = table_ref[rows:, :]
    zero = jnp.zeros((rows, 128), jnp.bfloat16)
    normed = normalized(x_ref)
    for p in range(inner // 128):
        if p % (NB // 128) == 0:
            k = 128 * p // NB
            part = block_dot(normed, copies, buffer, k).astype(jnp.bfloat16)
            q_ref[:, NB * k : NB * (k + 1)] = part
        at = 128 * p % NB
        queries = part[:, at : at + 128]
        keys = kv_ref[:, 128 * p : 128 * (p + 1)]
        values = kv_ref[:, inner + 128 * p : inner + 128 * (p + 1)]
        weights = []
        for k in range(2):
            h = 2 * p + k
            own = jnp.where(low, queries, zero) if k == 0 else jnp.where(low, zero, queries)
            scores = lax.dot_general(
                own, keys, (((1,), (1,)), ((), ())), preferred_element_type=jnp.float32
            )
            gap = cum[:, h : h + 1] - cum_t[h : h + 1, :]
            decay = jnp.exp(jnp.where(causal, gap, 0.0))
            weights.append(jnp.where(causal, scores * decay, 0.0).astype(jnp.bfloat16))
        both = jnp.concatenate(
            [jnp.where(low, values, zero), jnp.where(low, zero, values)], axis=0
        )
        out_ref[:, 128 * p : 128 * (p + 1)] = jnp.dot(
            jnp.concatenate(weights, axis=1), both, preferred_element_type=jnp.float32
        )


def within(x, weights, kv, table):
    rows, width = x.shape
    inner = kv.shape[1] // 2
    share = width // 64
    blocks = [(share, [(side, 0, 0, NB)]) for side in range(2)]
    vmem = pl.BlockSpec(memory_space=pltpu.VMEM)
    return pl.pallas_call(
        functools.partial(within_kernel, blocks),
        in_specs=[vmem, pl.BlockSpec(memory_space=pl.ANY), vmem, vmem],
        out_specs=[vmem] * 2,
        out_shape=[
            jax.ShapeDtypeStruct((rows, inner), jnp.bfloat16),
            jax.ShapeDtypeStruct((rows, inner), jnp.float32),
        ],
        scratch_shapes=[
            pltpu.VMEM((len(blocks), 2, 32, share, NB), jnp.bfloat16),
            pltpu.SemaphoreType.DMA((len(blocks), 2)),
        ],
        compiler_params=pltpu.CompilerParams(vmem_limit_bytes=VMEM_KEPT),
        cost_estimate=pl.CostEstimate(
            flops=2 * rows * width * inner + 6 * rows * rows * inner,
            bytes_accessed=2 * width * inner + 16 * rows * inner,
            transcendentals=16 * rows * rows,
        ),
        name="within",
    )(x, weights, kv, table)


def carry_kernel(start_ref, state_ref, total_ref, out_ref):
    carried = jnp.zeros(state_ref.shape[1:], jnp.float32)
    count = state_ref.shape[0]
    start = start_ref[0]
    for i in range(count):
        c = start + i if i < count // 2 else i - start
        out_ref[c] = carried.astype(jnp.bfloat16)
        carried = total_ref[pl.ds(c, 1), :] * carried + state_ref[c].astype(jnp.float32)


def carry(states, totals, start):
    return pl.pallas_call(
        carry_kernel,
        in_specs=[pl.BlockSpec(memory_space=pltpu.SMEM)] + [pl.BlockSpec(memory_space=pltpu.VMEM)] * 2,
        out_specs=pl.BlockSpec(memory_space=pltpu.VMEM),
        out_shape=jax.ShapeDtypeStruct(states.shape, jnp.bfloat16),
        compiler_params=pltpu.CompilerParams(vmem_limit_bytes=4 * 2**20),
        cost_estimate=pl.CostEstimate(
            flops=2 * states.size, bytes_accessed=4 * states.size, transcendentals=0
        ),
        name="carry",
    )(start, states, totals)


def output_kernel(
    blocks, q_ref, carried_ref, table_ref, within_ref, x_ref, w_ref, out_ref, buffer, sems
):
    copies = share_copies(blocks, w_ref, buffer, sems)
    start_all(copies)
    rows, inner = within_ref.shape
    low = half_mask(rows, 128, 64)
    low64 = low[:64]
    zero = jnp.zeros((64, 128), jnp.bfloat16)
    grow = table_ref[:rows, 32:48]
    mixed = []
    for p in range(inner // 128):
        cols = slice(128 * p, 128 * (p + 1))
        state = carried_ref[64 * p : 64 * (p + 1), :]
        both = jnp.concatenate(
            [jnp.where(low64, state, zero), jnp.where(low64, zero, state)], axis=0
        )
        earlier = jnp.dot(q_ref[:, cols], both, preferred_element_type=jnp.float32)
        mixture = within_ref[:, cols] + earlier * by_head(low, grow, p)
        square = mixture * mixture
        first = jnp.sum(jnp.where(low, square, 0.0), axis=-1, keepdims=True)
        second = jnp.sum(jnp.where(low, 0.0, square), axis=-1, keepdims=True)
        scale = jnp.where(
            low, lax.rsqrt(first * (1.0 / 64.0) + EPS), lax.rsqrt(second * (1.0 / 64.0) + EPS)
        )
        mixed.append((mixture * scale).astype(jnp.bfloat16))
    mixed = jnp.concatenate(mixed, axis=1)
    for k in range(len(blocks)):
        cols = slice(NB * k, NB * (k + 1))
        acc = block_dot(mixed, copies, buffer, k)
        out_ref[:, cols] = (x_ref[:, cols].astype(jnp.float32) + acc).astype(jnp.bfloat16)


def output(q, carried, table, inside, x, weights):
    rows, width = x.shape
    inner = inside.shape[1]
    share = inner // 64
    first = 3 * (width // 64)
    blocks = [(share, [(n // 2, first + share * (n % 2), 0, NB)]) for n in range(4)]
    vmem = pl.BlockSpec(memory_space=pltpu.VMEM)
    return pl.pallas_call(
        functools.partial(output_kernel, blocks),
        in_specs=[vmem] * 5 + [pl.BlockSpec(memory_space=pl.ANY)],
        out_specs=vmem,
        out_shape=jax.ShapeDtypeStruct((rows, width), jnp.bfloat16),
        scratch_shapes=[
            pltpu.VMEM((len(blocks), 2, 32, share, NB), jnp.bfloat16),
            pltpu.SemaphoreType.DMA((len(blocks), 2)),
        ],
        compiler_params=pltpu.CompilerParams(vmem_limit_bytes=VMEM_KEPT),
        cost_estimate=pl.CostEstimate(
            flops=2 * rows * width * inner, bytes_accessed=2 * width * inner, transcendentals=0
        ),
        name="output",
    )(q, carried, table, inside, x, weights)


def paired(low, high, core):
    keep = jnp.where(core == 0, low, high)
    other = swap(jnp.where(core == 0, high, low), "core")
    return jnp.where(core == 0, keep, other), jnp.where(core == 0, other, keep)


def across(value, axes):
    flip = [(0, 3), (1, 2), (2, 1), (3, 0)] if len(axes) == 2 else [(0, 1), (1, 0)]
    return lax.ppermute(value, axes, flip)


def hand_over(value, hops):
    pairs = []
    for level, turn in hops:
        for core in range(2):
            for far in range(2):
                goal = far ^ core if turn else far
                pairs.append((level * 4 + core * 2 + far, (1 - level) * 4 + core * 2 + goal))
    return lax.ppermute(value, ("ylo", "core", "yhi"), pairs)


def shared_weights(qkv, out, core, level):
    rows, depth = qkv.shape[0], out.shape[0]
    inner = qkv.shape[1] // 3
    halves = []
    for side in range(2):
        cut = [qkv[:, inner * i + NB * side : inner * i + NB * (side + 1)] for i in range(3)]
        first = out.shape[1] // 2 * side
        cut += [out[:, first + NB * i : first + NB * (i + 1)] for i in range(2)]
        halves.append(jnp.concatenate(cut, axis=0))
    first, second = paired(halves[0], halves[1], core)
    stay = jnp.where(level == 0, first, second)
    leave = jnp.where(level == 0, second, first)
    far = across(stay, ("yhi",))
    come, come_far = across(leave, ("ylo",)), across(leave, ("ylo", "yhi"))
    place = lax.axis_index("yhi")
    gathered = []
    for layer in range(2):
        staying = level == layer
        pair = jnp.where(staying, stay, come), jnp.where(staying, far, come_far)
        own = jnp.concatenate(
            [jnp.where(place == 0, pair[0], pair[1]), jnp.where(place == 0, pair[1], pair[0])], axis=0
        )
        gathered.append(lax.all_gather(own, SPREAD, axis=0).reshape(2, -1, own.shape[0], NB))
    return gathered


def decays(log_decay, core, level):
    first, second = paired(log_decay[0], log_decay[1], core)
    come = hand_over(jnp.where(level == 0, second, first), [(0, True), (1, False)])
    both = [jnp.where(level == 0, first, come), jnp.where(level == 0, come, second)]
    rows, heads = first.shape
    lower = jnp.tril(jnp.ones((rows, rows), jnp.float32))
    blocks = lax.axis_size(CTX)
    per_pair = blocks // (heads // 2)
    tables, rows_sent = [], []
    for d in both:
        cum = jnp.dot(lower, d, precision=lax.Precision.HIGHEST)
        ending = cum[-1:]
        total = jnp.exp(ending[0])
        lanes = jnp.repeat(total.reshape(heads // 2, 2), 64, axis=1)
        rows_sent.append(jnp.repeat(lanes, per_pair, axis=0))
        wide = jnp.concatenate([cum, jnp.exp(ending - cum), jnp.exp(cum)], axis=1)
        wide = jnp.pad(wide, ((0, 0), (0, rows - wide.shape[1])))
        tables.append(jnp.concatenate([wide, cum.T], axis=0))
    sent = jnp.stack(rows_sent + [jnp.zeros_like(rows_sent[0])] * 6, axis=1)
    received = lax.all_to_all(sent, CTX, 0, 0, tiled=True)
    return tables, [received[:, k, :] for k in range(2)]


def shards(tokens, qkv_weight, out_weight, log_decay):
    core = lax.axis_index("core")
    level = lax.axis_index("ylo")
    blocks = lax.axis_size(CTX)
    x = lax.dynamic_index_in_dim(tokens, core, 0, False)
    weights = shared_weights(qkv_weight[0], out_weight[0], core, level)
    tables, totals = decays(log_decay[0], core, level)
    x, totals, tables = lax.optimization_barrier((x, totals, tables))
    straight = jnp.zeros((1,), jnp.int32)
    turned = straight + core * (blocks // 2)
    kept = []
    for step in range(4):
        layer = step // 2
        table, w = tables[layer], weights[layer]
        if step > 0:
            x = hand_over(x, [(1 - step % 2, step < 3)])
            kept.append(x)
        kv, state = project_keys(x, w, table)
        slices = lax.all_to_all(state.reshape(blocks, -1, 128), CTX, 0, 0, tiled=True)
        q, inside = within(x, w, kv, table)
        slices, inside = lax.optimization_barrier((slices, inside))
        mine = carry(slices, totals[layer], turned if step == 1 else straight)
        carried = lax.all_to_all(mine, CTX, 0, 0, tiled=True).reshape(state.shape)
        x = output(q, carried, table, inside, x, w)
        kept.append(x)
    first = jnp.where(level == 0, kept[0], kept[5])
    second = jnp.where(level == 0, kept[3], kept[6])
    other = swap(jnp.where(core == 0, second, first), "core")
    result = jnp.stack([jnp.where(core == 0, first, other), jnp.where(core == 0, other, second)])
    return result[None]


def solution(mesh):
    fine = Mesh(mesh.devices.reshape(2, 2, 2, 4, 8), ("ylo", "core") + CTX)
    section = ("ylo", "core")
    in_specs = (
        P(None, CTX, None),
        P(section, CTX, None),
        P(section, CTX, None),
        P(section, None, CTX, None),
    )
    return jax.shard_map(
        shards, mesh=fine, in_specs=in_specs, out_specs=P(section, None, CTX, None), check_vma=False
    )
```

```python
import functools

import jax
import jax.numpy as jnp
from jax import lax
from jax.experimental import pallas as pl
from jax.experimental.pallas import tpu as pltpu
from jax.sharding import Mesh, PartitionSpec as P

CTX = ("yhi", "x", "z")
SPREAD = ("core", "x", "z")
NB = 512
EPS = 1e-05
VMEM_KEPT = 50 * 2**20


def swap(value, axis):
    return lax.ppermute(value, axis, [(0, 1), (1, 0)])


def half_mask(rows, lanes, half):
    return lax.broadcasted_iota(jnp.int32, (rows, lanes), 1) < half


def by_head(low, table, p):
    return jnp.where(low, table[:, 2 * p : 2 * p + 1], table[:, 2 * p + 1 : 2 * p + 2])


def share_copies(blocks, w_ref, buffer, sems):
    copies = []
    stride = w_ref.shape[2] // 2
    for k, (rows, parts) in enumerate(blocks):
        block, at = [], 0
        for side, first, column, count in parts:
            for far in range(2):
                source = w_ref.at[side, :, pl.ds(far * stride + first, rows), pl.ds(column, count)]
                goal = buffer.at[k, far, :, :, pl.ds(at, count)]
                block.append(pltpu.make_async_copy(source, goal, sems.at[k, len(block)]))
            at += count
        copies.append(block)
    return copies


def start_all(copies):
    for block in copies:
        for copy in block:
            copy.start()


def block_dot(left, copies, buffer, k):
    for copy in copies[k]:
        copy.wait()
    return jnp.dot(left, buffer[k].reshape(left.shape[1], NB), preferred_element_type=jnp.float32)


def normalized(x_ref):
    x = x_ref[...].astype(jnp.float32)
    return (x * lax.rsqrt(jnp.mean(x * x, axis=-1, keepdims=True) + EPS)).astype(jnp.bfloat16)


def fetch_kernel(blocks, w_ref, out_ref, sems):
    copies = share_copies(blocks, w_ref, out_ref, sems)
    start_all(copies)
    for block in copies:
        for copy in block:
            copy.wait()


def key_blocks(share):
    half = NB // 2
    return [
        (share, [(side, share * part, half * i, half) for part in (1, 2)])
        for side in range(2)
        for i in range(2)
    ]


def fetch_keys(weights, share):
    return pl.pallas_call(
        functools.partial(fetch_kernel, key_blocks(share)),
        in_specs=[pl.BlockSpec(memory_space=pl.ANY)],
        out_specs=pl.BlockSpec(memory_space=pltpu.VMEM),
        out_shape=pltpu.VMEM((4, 2, 32, share, NB), jnp.bfloat16),
        scratch_shapes=[pltpu.SemaphoreType.DMA((4, 4))],
        compiler_params=pltpu.CompilerParams(vmem_limit_bytes=VMEM_KEPT),
        cost_estimate=pl.CostEstimate(flops=0, bytes_accessed=4 * 4 * 64 * share * NB, transcendentals=0),
        name="fetch",
    )(weights)


def fetched_keys_kernel(x_ref, buffer, table_ref, kv_ref, state_ref):
    keys_of([[]] * buffer.shape[0], x_ref, table_ref, kv_ref, state_ref, buffer)


def keys_kernel(blocks, x_ref, w_ref, table_ref, kv_ref, state_ref, buffer, sems):
    copies = share_copies(blocks, w_ref, buffer, sems)
    start_all(copies)
    keys_of(copies, x_ref, table_ref, kv_ref, state_ref, buffer)


def keys_of(copies, x_ref, table_ref, kv_ref, state_ref, buffer):
    rows = x_ref.shape[0]
    inner = kv_ref.shape[1] // 2
    normed = normalized(x_ref)
    low = half_mask(rows, 128, 64)
    scale = table_ref[:rows, 16:32]
    half = NB // 2
    for k in range(len(copies)):
        part = block_dot(normed, copies, buffer, k).astype(jnp.bfloat16)
        kv_ref[:, half * k : half * (k + 1)] = part[:, :half]
        kv_ref[:, inner + half * k : inner + half * (k + 1)] = part[:, half:]
        for c in range(half // 128):
            p = half * k // 128 + c
            keys = part[:, 128 * c : 128 * (c + 1)].astype(jnp.float32) * by_head(low, scale, p)
            outer = lax.dot_general(
                keys.astype(jnp.bfloat16),
                part[:, half + 128 * c : half + 128 * (c + 1)],
                (((0,), (0,)), ((), ())),
                preferred_element_type=jnp.float32,
            )
            state_ref[64 * p : 64 * (p + 1), :] = jnp.where(
                low[:64], outer[:64], outer[64:]
            ).astype(jnp.bfloat16)


def project_keys(x, weights, table):
    rows, width = x.shape
    inner = 1024
    share = width // 64
    blocks = key_blocks(share)
    vmem = pl.BlockSpec(memory_space=pltpu.VMEM)
    fetched = weights.ndim == 5
    scratch = [
        pltpu.VMEM((len(blocks), 2, 32, share, NB), jnp.bfloat16),
        pltpu.SemaphoreType.DMA((len(blocks), 4)),
    ]
    return pl.pallas_call(
        fetched_keys_kernel if fetched else functools.partial(keys_kernel, blocks),
        in_specs=[vmem, vmem if fetched else pl.BlockSpec(memory_space=pl.ANY), vmem],
        out_specs=[vmem] * 2,
        out_shape=[
            jax.ShapeDtypeStruct((rows, 2 * inner), jnp.bfloat16),
            jax.ShapeDtypeStruct((inner // 2, 128), jnp.bfloat16),
        ],
        scratch_shapes=[] if fetched else scratch,
        compiler_params=pltpu.CompilerParams(vmem_limit_bytes=16 * 2**20 if fetched else VMEM_KEPT),
        cost_estimate=pl.CostEstimate(
            flops=4 * rows * width * inner, bytes_accessed=4 * width * inner, transcendentals=0
        ),
        name="keys",
    )(x, weights, table)


def within_kernel(blocks, x_ref, w_ref, kv_ref, table_ref, q_ref, out_ref, buffer, sems):
    copies = share_copies(blocks, w_ref, buffer, sems)
    start_all(copies)
    rows = kv_ref.shape[0]
    inner = kv_ref.shape[1] // 2
    low = half_mask(rows, 128, 64)
    causal = lax.broadcasted_iota(jnp.int32, (rows, rows), 0) >= lax.broadcasted_iota(
        jnp.int32, (rows, rows), 1
    )
    cum = table_ref[:rows, :16]
    cum_t = table_ref[rows:, :]
    zero = jnp.zeros((rows, 128), jnp.bfloat16)
    normed = normalized(x_ref)
    for p in range(inner // 128):
        if p % (NB // 128) == 0:
            k = 128 * p // NB
            part = block_dot(normed, copies, buffer, k).astype(jnp.bfloat16)
            q_ref[:, NB * k : NB * (k + 1)] = part
        at = 128 * p % NB
        queries = part[:, at : at + 128]
        keys = kv_ref[:, 128 * p : 128 * (p + 1)]
        values = kv_ref[:, inner + 128 * p : inner + 128 * (p + 1)]
        weights = []
        for k in range(2):
            h = 2 * p + k
            own = jnp.where(low, queries, zero) if k == 0 else jnp.where(low, zero, queries)
            scores = lax.dot_general(
                own, keys, (((1,), (1,)), ((), ())), preferred_element_type=jnp.float32
            )
            gap = cum[:, h : h + 1] - cum_t[h : h + 1, :]
            decay = jnp.exp(jnp.where(causal, gap, 0.0))
            weights.append(jnp.where(causal, scores * decay, 0.0).astype(jnp.bfloat16))
        both = jnp.concatenate(
            [jnp.where(low, values, zero), jnp.where(low, zero, values)], axis=0
        )
        out_ref[:, 128 * p : 128 * (p + 1)] = jnp.dot(
            jnp.concatenate(weights, axis=1), both, preferred_element_type=jnp.float32
        )


def within(x, weights, kv, table):
    rows, width = x.shape
    inner = kv.shape[1] // 2
    share = width // 64
    blocks = [(share, [(side, 0, 0, NB)]) for side in range(2)]
    vmem = pl.BlockSpec(memory_space=pltpu.VMEM)
    return pl.pallas_call(
        functools.partial(within_kernel, blocks),
        in_specs=[vmem, pl.BlockSpec(memory_space=pl.ANY), vmem, vmem],
        out_specs=[vmem] * 2,
        out_shape=[
            jax.ShapeDtypeStruct((rows, inner), jnp.bfloat16),
            jax.ShapeDtypeStruct((rows, inner), jnp.float32),
        ],
        scratch_shapes=[
            pltpu.VMEM((len(blocks), 2, 32, share, NB), jnp.bfloat16),
            pltpu.SemaphoreType.DMA((len(blocks), 2)),
        ],
        compiler_params=pltpu.CompilerParams(vmem_limit_bytes=VMEM_KEPT),
        cost_estimate=pl.CostEstimate(
            flops=2 * rows * width * inner + 6 * rows * rows * inner,
            bytes_accessed=2 * width * inner + 16 * rows * inner,
            transcendentals=16 * rows * rows,
        ),
        name="within",
    )(x, weights, kv, table)


def carry_kernel(start_ref, state_ref, total_ref, out_ref):
    carried = jnp.zeros(state_ref.shape[1:], jnp.float32)
    count = state_ref.shape[0]
    start = start_ref[0]
    for i in range(count):
        c = start + i if i < count // 2 else i - start
        out_ref[c] = carried.astype(jnp.bfloat16)
        carried = total_ref[pl.ds(c, 1), :] * carried + state_ref[c].astype(jnp.float32)


def carry(states, totals, start):
    return pl.pallas_call(
        carry_kernel,
        in_specs=[pl.BlockSpec(memory_space=pltpu.SMEM)] + [pl.BlockSpec(memory_space=pltpu.VMEM)] * 2,
        out_specs=pl.BlockSpec(memory_space=pltpu.VMEM),
        out_shape=jax.ShapeDtypeStruct(states.shape, jnp.bfloat16),
        compiler_params=pltpu.CompilerParams(vmem_limit_bytes=4 * 2**20),
        cost_estimate=pl.CostEstimate(
            flops=2 * states.size, bytes_accessed=4 * states.size, transcendentals=0
        ),
        name="carry",
    )(start, states, totals)


def output_kernel(
    blocks, q_ref, carried_ref, table_ref, within_ref, x_ref, w_ref, out_ref, buffer, sems
):
    copies = share_copies(blocks, w_ref, buffer, sems)
    start_all(copies)
    rows, inner = within_ref.shape
    low = half_mask(rows, 128, 64)
    low64 = low[:64]
    zero = jnp.zeros((64, 128), jnp.bfloat16)
    grow = table_ref[:rows, 32:48]
    mixed = []
    for p in range(inner // 128):
        cols = slice(128 * p, 128 * (p + 1))
        state = carried_ref[64 * p : 64 * (p + 1), :]
        both = jnp.concatenate(
            [jnp.where(low64, state, zero), jnp.where(low64, zero, state)], axis=0
        )
        earlier = jnp.dot(q_ref[:, cols], both, preferred_element_type=jnp.float32)
        mixture = within_ref[:, cols] + earlier * by_head(low, grow, p)
        square = mixture * mixture
        first = jnp.sum(jnp.where(low, square, 0.0), axis=-1, keepdims=True)
        second = jnp.sum(jnp.where(low, 0.0, square), axis=-1, keepdims=True)
        scale = jnp.where(
            low, lax.rsqrt(first * (1.0 / 64.0) + EPS), lax.rsqrt(second * (1.0 / 64.0) + EPS)
        )
        mixed.append((mixture * scale).astype(jnp.bfloat16))
    mixed = jnp.concatenate(mixed, axis=1)
    for k in range(len(blocks)):
        cols = slice(NB * k, NB * (k + 1))
        acc = block_dot(mixed, copies, buffer, k)
        out_ref[:, cols] = (x_ref[:, cols].astype(jnp.float32) + acc).astype(jnp.bfloat16)


def output(q, carried, table, inside, x, weights):
    rows, width = x.shape
    inner = inside.shape[1]
    share = inner // 64
    first = 3 * (width // 64)
    blocks = [(share, [(n // 2, first + share * (n % 2), 0, NB)]) for n in range(4)]
    vmem = pl.BlockSpec(memory_space=pltpu.VMEM)
    return pl.pallas_call(
        functools.partial(output_kernel, blocks),
        in_specs=[vmem] * 5 + [pl.BlockSpec(memory_space=pl.ANY)],
        out_specs=vmem,
        out_shape=jax.ShapeDtypeStruct((rows, width), jnp.bfloat16),
        scratch_shapes=[
            pltpu.VMEM((len(blocks), 2, 32, share, NB), jnp.bfloat16),
            pltpu.SemaphoreType.DMA((len(blocks), 2)),
        ],
        compiler_params=pltpu.CompilerParams(vmem_limit_bytes=VMEM_KEPT),
        cost_estimate=pl.CostEstimate(
            flops=2 * rows * width * inner, bytes_accessed=2 * width * inner, transcendentals=0
        ),
        name="output",
    )(q, carried, table, inside, x, weights)


def paired(low, high, core):
    keep = jnp.where(core == 0, low, high)
    other = swap(jnp.where(core == 0, high, low), "core")
    return jnp.where(core == 0, keep, other), jnp.where(core == 0, other, keep)


def across(value, axes):
    flip = [(0, 3), (1, 2), (2, 1), (3, 0)] if len(axes) == 2 else [(0, 1), (1, 0)]
    return lax.ppermute(value, axes, flip)


def split_kernel(core_ref, qkv_ref, out_ref, keep_ref, give_ref):
    rows, depth = qkv_ref.shape[0], out_ref.shape[0]
    inner, wide = qkv_ref.shape[1] // 3, out_ref.shape[1] // 2
    core = core_ref[0]
    for side in range(2):
        for mine, goal in ((True, keep_ref), (False, give_ref)):

            @pl.when((core == side) == mine)
            def _(side=side, goal=goal):
                for i in range(3):
                    at = inner * i + NB * side
                    goal[rows * i : rows * (i + 1), :] = qkv_ref[:, at : at + NB]
                for i in range(2):
                    at, row = wide * side + NB * i, 3 * rows + depth * i
                    goal[row : row + depth, :] = out_ref[:, at : at + NB]


def split_halves(qkv, out, core):
    vmem = pl.BlockSpec(memory_space=pltpu.VMEM)
    half = jax.ShapeDtypeStruct(((qkv.size + out.size) // (2 * NB), NB), jnp.bfloat16)
    return pl.pallas_call(
        split_kernel,
        in_specs=[pl.BlockSpec(memory_space=pltpu.SMEM), vmem, vmem],
        out_specs=[vmem] * 2,
        out_shape=[half] * 2,
        compiler_params=pltpu.CompilerParams(vmem_limit_bytes=VMEM_KEPT),
        name="split",
    )(core.reshape(1).astype(jnp.int32), qkv, out)


def hand_over(value, hops):
    pairs = []
    for level, turn in hops:
        for core in range(2):
            for far in range(2):
                goal = far ^ core if turn else far
                pairs.append((level * 4 + core * 2 + far, (1 - level) * 4 + core * 2 + goal))
    return lax.ppermute(value, ("ylo", "core", "yhi"), pairs)


def shared_weights(qkv, out, core, level):
    keep, give = split_halves(qkv, out, core)
    other = swap(give, "core")
    first, second = jnp.where(core == 0, keep, other), jnp.where(core == 0, other, keep)
    stay = jnp.where(level == 0, first, second)
    leave = jnp.where(level == 0, second, first)
    far = across(stay, ("yhi",))
    come, come_far = across(leave, ("ylo",)), across(leave, ("ylo", "yhi"))
    place = lax.axis_index("yhi")
    gathered = []
    for layer in range(2):
        staying = level == layer
        pair = jnp.where(staying, stay, come), jnp.where(staying, far, come_far)
        own = jnp.concatenate(
            [jnp.where(place == 0, pair[0], pair[1]), jnp.where(place == 0, pair[1], pair[0])], axis=0
        )
        gathered.append(lax.all_gather(own, SPREAD, axis=0).reshape(2, -1, own.shape[0], NB))
    return gathered


def decays(log_decay, core, level):
    first, second = paired(log_decay[0], log_decay[1], core)
    come = hand_over(jnp.where(level == 0, second, first), [(0, True), (1, False)])
    both = [jnp.where(level == 0, first, come), jnp.where(level == 0, come, second)]
    rows, heads = first.shape
    lower = jnp.tril(jnp.ones((rows, rows), jnp.float32))
    blocks = lax.axis_size(CTX)
    per_pair = blocks // (heads // 2)
    tables, rows_sent = [], []
    for d in both:
        cum = jnp.dot(lower, d, precision=lax.Precision.HIGHEST)
        ending = cum[-1:]
        total = jnp.exp(ending[0])
        lanes = jnp.repeat(total.reshape(heads // 2, 2), 64, axis=1)
        rows_sent.append(jnp.repeat(lanes, per_pair, axis=0))
        wide = jnp.concatenate([cum, jnp.exp(ending - cum), jnp.exp(cum)], axis=1)
        wide = jnp.pad(wide, ((0, 0), (0, rows - wide.shape[1])))
        tables.append(jnp.concatenate([wide, cum.T], axis=0))
    sent = jnp.stack(rows_sent + [jnp.zeros_like(rows_sent[0])] * 6, axis=1)
    received = lax.all_to_all(sent, CTX, 0, 0, tiled=True)
    return tables, [received[:, k, :] for k in range(2)]


def shards(tokens, qkv_weight, out_weight, log_decay):
    core = lax.axis_index("core")
    level = lax.axis_index("ylo")
    blocks = lax.axis_size(CTX)
    x = lax.dynamic_index_in_dim(tokens, core, 0, False)
    weights = shared_weights(qkv_weight[0], out_weight[0], core, level)
    tables, totals = decays(log_decay[0], core, level)
    x, totals, tables = lax.optimization_barrier((x, totals, tables))
    straight = jnp.zeros((1,), jnp.int32)
    turned = straight + core * (blocks // 2)
    kept = []
    for step in range(4):
        layer = step // 2
        table, w = tables[layer], weights[layer]
        keys_from = w
        if step > 0:
            _, source = lax.optimization_barrier((x, w))
            keys_from = fetch_keys(source, x.shape[1] // 64)
            x = hand_over(x, [(1 - step % 2, step < 3)])
            kept.append(x)
        kv, state = project_keys(x, keys_from, table)
        slices = lax.all_to_all(state.reshape(blocks, -1, 128), CTX, 0, 0, tiled=True)
        q, inside = within(x, w, kv, table)
        slices, inside = lax.optimization_barrier((slices, inside))
        mine = carry(slices, totals[layer], turned if step == 1 else straight)
        carried = lax.all_to_all(mine, CTX, 0, 0, tiled=True).reshape(state.shape)
        x = output(q, carried, table, inside, x, w)
        kept.append(x)
    first = jnp.where(level == 0, kept[0], kept[5])
    second = jnp.where(level == 0, kept[3], kept[6])
    other = swap(jnp.where(core == 0, second, first), "core")
    result = jnp.stack([jnp.where(core == 0, first, other), jnp.where(core == 0, other, second)])
    return result[None]


def solution(mesh):
    fine = Mesh(mesh.devices.reshape(2, 2, 2, 4, 8), ("ylo", "core") + CTX)
    section = ("ylo", "core")
    in_specs = (
        P(None, CTX, None),
        P(section, CTX, None),
        P(section, CTX, None),
        P(section, None, CTX, None),
    )
    return jax.shard_map(
        shards, mesh=fine, in_specs=in_specs, out_specs=P(section, None, CTX, None), check_vma=False
    )
```

```python
import functools

import jax
import jax.numpy as jnp
from jax import lax
from jax.experimental import pallas as pl
from jax.experimental.pallas import tpu as pltpu
from jax.sharding import Mesh, PartitionSpec as P

CTX = ("yhi", "x", "z")
SPREAD = ("core", "x", "z")
NB = 512
EPS = 1e-05
VMEM_KEPT = 50 * 2**20


def swap(value, axis):
    return lax.ppermute(value, axis, [(0, 1), (1, 0)])


def half_mask(rows, lanes, half):
    return lax.broadcasted_iota(jnp.int32, (rows, lanes), 1) < half


def by_head(low, table, p):
    return jnp.where(low, table[:, 2 * p : 2 * p + 1], table[:, 2 * p + 1 : 2 * p + 2])


def share_copies(blocks, w_ref, buffer, sems):
    copies = []
    stride = w_ref.shape[2] // 2
    for k, (rows, parts) in enumerate(blocks):
        block, at = [], 0
        for side, first, column, count in parts:
            for far in range(2):
                source = w_ref.at[side, :, pl.ds(far * stride + first, rows), pl.ds(column, count)]
                goal = buffer.at[k, far, :, :, pl.ds(at, count)]
                block.append(pltpu.make_async_copy(source, goal, sems.at[k, len(block)]))
            at += count
        copies.append(block)
    return copies


def start_all(copies):
    for block in copies:
        for copy in block:
            copy.start()


def block_dot(left, copies, buffer, k):
    for copy in copies[k]:
        copy.wait()
    return jnp.dot(left, buffer[k].reshape(left.shape[1], NB), preferred_element_type=jnp.float32)


def normalized(x_ref):
    x = x_ref[...].astype(jnp.float32)
    return (x * lax.rsqrt(jnp.mean(x * x, axis=-1, keepdims=True) + EPS)).astype(jnp.bfloat16)


def fetch_kernel(blocks, w_ref, out_ref, sems):
    copies = share_copies(blocks, w_ref, out_ref, sems)
    start_all(copies)
    for block in copies:
        for copy in block:
            copy.wait()


def key_blocks(share):
    half = NB // 2
    return [
        (share, [(side, share * part, half * i, half) for part in (1, 2)])
        for side in range(2)
        for i in range(2)
    ]


def fetch_keys(weights, share):
    return pl.pallas_call(
        functools.partial(fetch_kernel, key_blocks(share)),
        in_specs=[pl.BlockSpec(memory_space=pl.ANY)],
        out_specs=pl.BlockSpec(memory_space=pltpu.VMEM),
        out_shape=pltpu.VMEM((4, 2, 32, share, NB), jnp.bfloat16),
        scratch_shapes=[pltpu.SemaphoreType.DMA((4, 4))],
        compiler_params=pltpu.CompilerParams(vmem_limit_bytes=VMEM_KEPT),
        cost_estimate=pl.CostEstimate(flops=0, bytes_accessed=4 * 4 * 64 * share * NB, transcendentals=0),
        name="fetch",
    )(weights)


def fetched_keys_kernel(x_ref, buffer, table_ref, kv_ref, state_ref):
    keys_of([[]] * buffer.shape[0], x_ref, table_ref, kv_ref, state_ref, buffer)


def keys_kernel(blocks, x_ref, w_ref, table_ref, kv_ref, state_ref, buffer, sems):
    copies = share_copies(blocks, w_ref, buffer, sems)
    start_all(copies)
    keys_of(copies, x_ref, table_ref, kv_ref, state_ref, buffer)


def keys_of(copies, x_ref, table_ref, kv_ref, state_ref, buffer):
    rows = x_ref.shape[0]
    inner = kv_ref.shape[1] // 2
    normed = normalized(x_ref)
    low = half_mask(rows, 128, 64)
    scale = table_ref[:rows, 16:32]
    half = NB // 2
    for k in range(len(copies)):
        part = block_dot(normed, copies, buffer, k).astype(jnp.bfloat16)
        kv_ref[:, half * k : half * (k + 1)] = part[:, :half]
        kv_ref[:, inner + half * k : inner + half * (k + 1)] = part[:, half:]
        for c in range(half // 128):
            p = half * k // 128 + c
            keys = part[:, 128 * c : 128 * (c + 1)].astype(jnp.float32) * by_head(low, scale, p)
            outer = lax.dot_general(
                keys.astype(jnp.bfloat16),
                part[:, half + 128 * c : half + 128 * (c + 1)],
                (((0,), (0,)), ((), ())),
                preferred_element_type=jnp.float32,
            )
            state_ref[64 * p : 64 * (p + 1), :] = jnp.where(
                low[:64], outer[:64], outer[64:]
            ).astype(jnp.bfloat16)


def project_keys(x, weights, table):
    rows, width = x.shape
    inner = 1024
    share = width // 64
    blocks = key_blocks(share)
    vmem = pl.BlockSpec(memory_space=pltpu.VMEM)
    fetched = weights.ndim == 5
    scratch = [
        pltpu.VMEM((len(blocks), 2, 32, share, NB), jnp.bfloat16),
        pltpu.SemaphoreType.DMA((len(blocks), 4)),
    ]
    return pl.pallas_call(
        fetched_keys_kernel if fetched else functools.partial(keys_kernel, blocks),
        in_specs=[vmem, vmem if fetched else pl.BlockSpec(memory_space=pl.ANY), vmem],
        out_specs=[vmem] * 2,
        out_shape=[
            jax.ShapeDtypeStruct((rows, 2 * inner), jnp.bfloat16),
            jax.ShapeDtypeStruct((inner // 2, 128), jnp.bfloat16),
        ],
        scratch_shapes=[] if fetched else scratch,
        compiler_params=pltpu.CompilerParams(vmem_limit_bytes=16 * 2**20 if fetched else VMEM_KEPT),
        cost_estimate=pl.CostEstimate(
            flops=4 * rows * width * inner, bytes_accessed=4 * width * inner, transcendentals=0
        ),
        name="keys",
    )(x, weights, table)


def within_kernel(blocks, x_ref, w_ref, kv_ref, table_ref, q_ref, out_ref, buffer, sems):
    copies = share_copies(blocks, w_ref, buffer, sems)
    start_all(copies)
    rows = kv_ref.shape[0]
    inner = kv_ref.shape[1] // 2
    low = half_mask(rows, 128, 64)
    causal = lax.broadcasted_iota(jnp.int32, (rows, rows), 0) >= lax.broadcasted_iota(
        jnp.int32, (rows, rows), 1
    )
    cum = table_ref[:rows, :16]
    cum_t = table_ref[rows:, :]
    zero = jnp.zeros((rows, 128), jnp.bfloat16)
    normed = normalized(x_ref)
    for p in range(inner // 128):
        if p % (NB // 128) == 0:
            k = 128 * p // NB
            part = block_dot(normed, copies, buffer, k).astype(jnp.bfloat16)
            q_ref[:, NB * k : NB * (k + 1)] = part
        at = 128 * p % NB
        queries = part[:, at : at + 128]
        keys = kv_ref[:, 128 * p : 128 * (p + 1)]
        values = kv_ref[:, inner + 128 * p : inner + 128 * (p + 1)]
        weights = []
        for k in range(2):
            h = 2 * p + k
            own = jnp.where(low, queries, zero) if k == 0 else jnp.where(low, zero, queries)
            scores = lax.dot_general(
                own, keys, (((1,), (1,)), ((), ())), preferred_element_type=jnp.float32
            )
            gap = cum[:, h : h + 1] - cum_t[h : h + 1, :]
            decay = jnp.exp(jnp.where(causal, gap, 0.0))
            weights.append(jnp.where(causal, scores * decay, 0.0).astype(jnp.bfloat16))
        both = jnp.concatenate(
            [jnp.where(low, values, zero), jnp.where(low, zero, values)], axis=0
        )
        out_ref[:, 128 * p : 128 * (p + 1)] = jnp.dot(
            jnp.concatenate(weights, axis=1), both, preferred_element_type=jnp.float32
        )


def within(x, weights, kv, table):
    rows, width = x.shape
    inner = kv.shape[1] // 2
    share = width // 64
    blocks = [(share, [(side, 0, 0, NB)]) for side in range(2)]
    vmem = pl.BlockSpec(memory_space=pltpu.VMEM)
    return pl.pallas_call(
        functools.partial(within_kernel, blocks),
        in_specs=[vmem, pl.BlockSpec(memory_space=pl.ANY), vmem, vmem],
        out_specs=[vmem] * 2,
        out_shape=[
            jax.ShapeDtypeStruct((rows, inner), jnp.bfloat16),
            jax.ShapeDtypeStruct((rows, inner), jnp.float32),
        ],
        scratch_shapes=[
            pltpu.VMEM((len(blocks), 2, 32, share, NB), jnp.bfloat16),
            pltpu.SemaphoreType.DMA((len(blocks), 2)),
        ],
        compiler_params=pltpu.CompilerParams(vmem_limit_bytes=VMEM_KEPT),
        cost_estimate=pl.CostEstimate(
            flops=2 * rows * width * inner + 6 * rows * rows * inner,
            bytes_accessed=2 * width * inner + 16 * rows * inner,
            transcendentals=16 * rows * rows,
        ),
        name="within",
    )(x, weights, kv, table)


def carry_kernel(start_ref, state_ref, total_ref, out_ref):
    carried = jnp.zeros(state_ref.shape[1:], jnp.float32)
    count = state_ref.shape[0]
    start = start_ref[0]
    for i in range(count):
        c = start + i if i < count // 2 else i - start
        out_ref[c] = carried.astype(jnp.bfloat16)
        carried = total_ref[pl.ds(c, 1), :] * carried + state_ref[c].astype(jnp.float32)


def carry(states, totals, start):
    return pl.pallas_call(
        carry_kernel,
        in_specs=[pl.BlockSpec(memory_space=pltpu.SMEM)] + [pl.BlockSpec(memory_space=pltpu.VMEM)] * 2,
        out_specs=pl.BlockSpec(memory_space=pltpu.VMEM),
        out_shape=jax.ShapeDtypeStruct(states.shape, jnp.bfloat16),
        compiler_params=pltpu.CompilerParams(vmem_limit_bytes=4 * 2**20),
        cost_estimate=pl.CostEstimate(
            flops=2 * states.size, bytes_accessed=4 * states.size, transcendentals=0
        ),
        name="carry",
    )(start, states, totals)


def output_kernel(
    blocks, q_ref, carried_ref, table_ref, within_ref, x_ref, w_ref, out_ref, buffer, sems
):
    copies = share_copies(blocks, w_ref, buffer, sems)
    start_all(copies)
    rows, inner = within_ref.shape
    low = half_mask(rows, 128, 64)
    low64 = low[:64]
    zero = jnp.zeros((64, 128), jnp.bfloat16)
    grow = table_ref[:rows, 32:48]
    mixed = []
    for p in range(inner // 128):
        cols = slice(128 * p, 128 * (p + 1))
        state = carried_ref[64 * p : 64 * (p + 1), :]
        both = jnp.concatenate(
            [jnp.where(low64, state, zero), jnp.where(low64, zero, state)], axis=0
        )
        earlier = jnp.dot(q_ref[:, cols], both, preferred_element_type=jnp.float32)
        mixture = within_ref[:, cols] + earlier * by_head(low, grow, p)
        square = mixture * mixture
        first = jnp.sum(jnp.where(low, square, 0.0), axis=-1, keepdims=True)
        second = jnp.sum(jnp.where(low, 0.0, square), axis=-1, keepdims=True)
        scale = jnp.where(
            low, lax.rsqrt(first * (1.0 / 64.0) + EPS), lax.rsqrt(second * (1.0 / 64.0) + EPS)
        )
        mixed.append((mixture * scale).astype(jnp.bfloat16))
    mixed = jnp.concatenate(mixed, axis=1)
    for k in range(len(blocks)):
        cols = slice(NB * k, NB * (k + 1))
        acc = block_dot(mixed, copies, buffer, k)
        out_ref[:, cols] = (x_ref[:, cols].astype(jnp.float32) + acc).astype(jnp.bfloat16)


def output(q, carried, table, inside, x, weights):
    rows, width = x.shape
    inner = inside.shape[1]
    share = inner // 64
    first = 3 * (width // 64)
    blocks = [(share, [(n // 2, first + share * (n % 2), 0, NB)]) for n in range(4)]
    vmem = pl.BlockSpec(memory_space=pltpu.VMEM)
    return pl.pallas_call(
        functools.partial(output_kernel, blocks),
        in_specs=[vmem] * 5 + [pl.BlockSpec(memory_space=pl.ANY)],
        out_specs=vmem,
        out_shape=jax.ShapeDtypeStruct((rows, width), jnp.bfloat16),
        scratch_shapes=[
            pltpu.VMEM((len(blocks), 2, 32, share, NB), jnp.bfloat16),
            pltpu.SemaphoreType.DMA((len(blocks), 2)),
        ],
        compiler_params=pltpu.CompilerParams(vmem_limit_bytes=VMEM_KEPT),
        cost_estimate=pl.CostEstimate(
            flops=2 * rows * width * inner, bytes_accessed=2 * width * inner, transcendentals=0
        ),
        name="output",
    )(q, carried, table, inside, x, weights)


def paired(low, high, core):
    keep = jnp.where(core == 0, low, high)
    other = swap(jnp.where(core == 0, high, low), "core")
    return jnp.where(core == 0, keep, other), jnp.where(core == 0, other, keep)


def across(value, axes):
    flip = [(0, 3), (1, 2), (2, 1), (3, 0)] if len(axes) == 2 else [(0, 1), (1, 0)]
    return lax.ppermute(value, axes, flip)


def split_kernel(core_ref, qkv_ref, out_ref, keep_ref, give_ref):
    rows, depth = qkv_ref.shape[0], out_ref.shape[0]
    inner, wide = qkv_ref.shape[1] // 3, out_ref.shape[1] // 2
    core = core_ref[0]
    for side in range(2):
        for mine, goal in ((True, keep_ref), (False, give_ref)):

            @pl.when((core == side) == mine)
            def _(side=side, goal=goal):
                for i in range(3):
                    at = inner * i + NB * side
                    goal[rows * i : rows * (i + 1), :] = qkv_ref[:, at : at + NB]
                for i in range(2):
                    at, row = wide * side + NB * i, 3 * rows + depth * i
                    goal[row : row + depth, :] = out_ref[:, at : at + NB]


def split_halves(qkv, out, core):
    vmem = pl.BlockSpec(memory_space=pltpu.VMEM)
    half = jax.ShapeDtypeStruct(((qkv.size + out.size) // (2 * NB), NB), jnp.bfloat16)
    return pl.pallas_call(
        split_kernel,
        in_specs=[pl.BlockSpec(memory_space=pltpu.SMEM), vmem, vmem],
        out_specs=[vmem] * 2,
        out_shape=[half] * 2,
        compiler_params=pltpu.CompilerParams(vmem_limit_bytes=VMEM_KEPT),
        name="split",
    )(core.reshape(1).astype(jnp.int32), qkv, out)


def hand_over(value, hops):
    pairs = []
    for level, turn in hops:
        for core in range(2):
            for far in range(2):
                goal = far ^ core if turn else far
                pairs.append((level * 4 + core * 2 + far, (1 - level) * 4 + core * 2 + goal))
    return lax.ppermute(value, ("ylo", "core", "yhi"), pairs)


def shared_weights(qkv, out, core, level):
    keep, give = split_halves(qkv, out, core)
    other = swap(give, "core")
    first, second = jnp.where(core == 0, keep, other), jnp.where(core == 0, other, keep)
    stay = jnp.where(level == 0, first, second)
    leave = jnp.where(level == 0, second, first)
    far = across(stay, ("yhi",))
    come, come_far = across(leave, ("ylo",)), across(leave, ("ylo", "yhi"))
    place = lax.axis_index("yhi")
    gathered = []
    for layer in range(2):
        staying = level == layer
        pair = jnp.where(staying, stay, come), jnp.where(staying, far, come_far)
        own = jnp.concatenate(
            [jnp.where(place == 0, pair[0], pair[1]), jnp.where(place == 0, pair[1], pair[0])], axis=0
        )
        gathered.append(lax.all_gather(own, SPREAD, axis=0).reshape(2, -1, own.shape[0], NB))
    return gathered


def decays(log_decay, core, level):
    first, second = paired(log_decay[0], log_decay[1], core)
    come = hand_over(jnp.where(level == 0, second, first), [(0, True), (1, False)])
    both = [jnp.where(level == 0, first, come), jnp.where(level == 0, come, second)]
    rows, heads = first.shape
    lower = jnp.tril(jnp.ones((rows, rows), jnp.float32))
    blocks = lax.axis_size(CTX)
    per_pair = blocks // (heads // 2)
    tables, rows_sent = [], []
    for d in both:
        cum = jnp.dot(lower, d, precision=lax.Precision.HIGHEST)
        ending = cum[-1:]
        total = jnp.exp(ending[0])
        lanes = jnp.repeat(total.reshape(heads // 2, 2), 64, axis=1)
        rows_sent.append(jnp.repeat(lanes, per_pair, axis=0))
        wide = jnp.concatenate([cum, jnp.exp(ending - cum), jnp.exp(cum)], axis=1)
        wide = jnp.pad(wide, ((0, 0), (0, rows - wide.shape[1])))
        tables.append(jnp.concatenate([wide, cum.T], axis=0))
    sent = jnp.stack(rows_sent, axis=1)
    received = lax.all_to_all(sent, CTX, 0, 0, tiled=True)
    return tables, [received[:, k, :] for k in range(2)]


def shards(tokens, qkv_weight, out_weight, log_decay):
    core = lax.axis_index("core")
    level = lax.axis_index("ylo")
    blocks = lax.axis_size(CTX)
    x = lax.dynamic_index_in_dim(tokens, core, 0, False)
    weights = shared_weights(qkv_weight[0], out_weight[0], core, level)
    tables, totals = decays(log_decay[0], core, level)
    x, totals, tables = lax.optimization_barrier((x, totals, tables))
    straight = jnp.zeros((1,), jnp.int32)
    turned = straight + core * (blocks // 2)
    kept = []
    for step in range(4):
        layer = step // 2
        table, w = tables[layer], weights[layer]
        keys_from = w
        if step > 0:
            _, source = lax.optimization_barrier((x, w))
            keys_from = fetch_keys(source, x.shape[1] // 64)
            x = hand_over(x, [(1 - step % 2, step < 3)])
            kept.append(x)
        kv, state = project_keys(x, keys_from, table)
        slices = lax.all_to_all(state.reshape(blocks, -1, 128), CTX, 0, 0, tiled=True)
        q, inside = within(x, w, kv, table)
        slices, inside = lax.optimization_barrier((slices, inside))
        mine = carry(slices, totals[layer], turned if step == 1 else straight)
        carried = lax.all_to_all(mine, CTX, 0, 0, tiled=True).reshape(state.shape)
        x = output(q, carried, table, inside, x, w)
        kept.append(x)
    first = jnp.where(level == 0, kept[0], kept[5])
    second = jnp.where(level == 0, kept[3], kept[6])
    other = swap(jnp.where(core == 0, second, first), "core")
    result = jnp.stack([jnp.where(core == 0, first, other), jnp.where(core == 0, other, second)])
    return result[None]


def solution(mesh):
    fine = Mesh(mesh.devices.reshape(2, 2, 2, 4, 8), ("ylo", "core") + CTX)
    section = ("ylo", "core")
    in_specs = (
        P(None, CTX, None),
        P(section, CTX, None),
        P(section, CTX, None),
        P(section, None, CTX, None),
    )
    return jax.shard_map(
        shards, mesh=fine, in_specs=in_specs, out_specs=P(section, None, CTX, None), check_vma=False
    )
```

```python
import functools

import jax
import jax.numpy as jnp
from jax import lax
from jax.experimental import pallas as pl
from jax.experimental.pallas import tpu as pltpu
from jax.sharding import Mesh, PartitionSpec as P

CTX = ("yhi", "x", "z")
SPREAD = ("x", "z", "core")
NB = 512
EPS = 1e-05
VMEM_KEPT = 50 * 2**20


def swap(value, axis):
    return lax.ppermute(value, axis, [(0, 1), (1, 0)])


def half_mask(rows, lanes, half):
    return lax.broadcasted_iota(jnp.int32, (rows, lanes), 1) < half


def by_head(low, table, p):
    return jnp.where(low, table[:, 2 * p : 2 * p + 1], table[:, 2 * p + 1 : 2 * p + 2])


def share_copies(blocks, w_ref, buffer, sems):
    copies = []
    stride = w_ref.shape[2] // 2
    for k, (rows, parts) in enumerate(blocks):
        block, at = [], 0
        for side, first, column, count in parts:
            for far in range(2):
                source = w_ref.at[:, side, pl.ds(far * stride + first, rows), pl.ds(column, count)]
                goal = buffer.at[k, far, :, :, pl.ds(at, count)]
                block.append(pltpu.make_async_copy(source, goal, sems.at[k, len(block)]))
            at += count
        copies.append(block)
    return copies


def start_all(copies):
    for block in copies:
        for copy in block:
            copy.start()


def block_dot(left, copies, buffer, k):
    for copy in copies[k]:
        copy.wait()
    return jnp.dot(left, buffer[k].reshape(left.shape[1], NB), preferred_element_type=jnp.float32)


def normalized(x_ref):
    x = x_ref[...].astype(jnp.float32)
    return (x * lax.rsqrt(jnp.mean(x * x, axis=-1, keepdims=True) + EPS)).astype(jnp.bfloat16)


def fetch_kernel(blocks, w_ref, out_ref, sems):
    copies = share_copies(blocks, w_ref, out_ref, sems)
    start_all(copies)
    for block in copies:
        for copy in block:
            copy.wait()


def key_blocks(share):
    half = NB // 2
    return [
        (share, [(side, share * part, half * i, half) for part in (1, 2)])
        for side in range(2)
        for i in range(2)
    ]


def fetch_keys(weights, share):
    return pl.pallas_call(
        functools.partial(fetch_kernel, key_blocks(share)),
        in_specs=[pl.BlockSpec(memory_space=pl.ANY)],
        out_specs=pl.BlockSpec(memory_space=pltpu.VMEM),
        out_shape=pltpu.VMEM((4, 2, 32, share, NB), jnp.bfloat16),
        scratch_shapes=[pltpu.SemaphoreType.DMA((4, 4))],
        compiler_params=pltpu.CompilerParams(vmem_limit_bytes=VMEM_KEPT),
        cost_estimate=pl.CostEstimate(flops=0, bytes_accessed=4 * 4 * 64 * share * NB, transcendentals=0),
        name="fetch",
    )(weights)


def fetched_keys_kernel(x_ref, buffer, table_ref, kv_ref, state_ref):
    keys_of([[]] * buffer.shape[0], x_ref, table_ref, kv_ref, state_ref, buffer)


def keys_kernel(blocks, x_ref, w_ref, table_ref, kv_ref, state_ref, buffer, sems):
    copies = share_copies(blocks, w_ref, buffer, sems)
    start_all(copies)
    keys_of(copies, x_ref, table_ref, kv_ref, state_ref, buffer)


def keys_of(copies, x_ref, table_ref, kv_ref, state_ref, buffer):
    rows = x_ref.shape[0]
    inner = kv_ref.shape[1] // 2
    normed = normalized(x_ref)
    low = half_mask(rows, 128, 64)
    scale = table_ref[:rows, 16:32]
    half = NB // 2
    for k in range(len(copies)):
        part = block_dot(normed, copies, buffer, k).astype(jnp.bfloat16)
        kv_ref[:, half * k : half * (k + 1)] = part[:, :half]
        kv_ref[:, inner + half * k : inner + half * (k + 1)] = part[:, half:]
        for c in range(half // 128):
            p = half * k // 128 + c
            keys = part[:, 128 * c : 128 * (c + 1)].astype(jnp.float32) * by_head(low, scale, p)
            outer = lax.dot_general(
                keys.astype(jnp.bfloat16),
                part[:, half + 128 * c : half + 128 * (c + 1)],
                (((0,), (0,)), ((), ())),
                preferred_element_type=jnp.float32,
            )
            state_ref[64 * p : 64 * (p + 1), :] = jnp.where(
                low[:64], outer[:64], outer[64:]
            ).astype(jnp.bfloat16)


def project_keys(x, weights, table):
    rows, width = x.shape
    inner = 1024
    share = width // 64
    blocks = key_blocks(share)
    vmem = pl.BlockSpec(memory_space=pltpu.VMEM)
    fetched = weights.ndim == 5
    scratch = [
        pltpu.VMEM((len(blocks), 2, 32, share, NB), jnp.bfloat16),
        pltpu.SemaphoreType.DMA((len(blocks), 4)),
    ]
    return pl.pallas_call(
        fetched_keys_kernel if fetched else functools.partial(keys_kernel, blocks),
        in_specs=[vmem, vmem if fetched else pl.BlockSpec(memory_space=pl.ANY), vmem],
        out_specs=[vmem] * 2,
        out_shape=[
            jax.ShapeDtypeStruct((rows, 2 * inner), jnp.bfloat16),
            jax.ShapeDtypeStruct((inner // 2, 128), jnp.bfloat16),
        ],
        scratch_shapes=[] if fetched else scratch,
        compiler_params=pltpu.CompilerParams(vmem_limit_bytes=16 * 2**20 if fetched else VMEM_KEPT),
        cost_estimate=pl.CostEstimate(
            flops=4 * rows * width * inner, bytes_accessed=4 * width * inner, transcendentals=0
        ),
        name="keys",
    )(x, weights, table)


def within_kernel(blocks, x_ref, w_ref, kv_ref, table_ref, q_ref, out_ref, buffer, sems):
    copies = share_copies(blocks, w_ref, buffer, sems)
    start_all(copies)
    rows = kv_ref.shape[0]
    inner = kv_ref.shape[1] // 2
    low = half_mask(rows, 128, 64)
    causal = lax.broadcasted_iota(jnp.int32, (rows, rows), 0) >= lax.broadcasted_iota(
        jnp.int32, (rows, rows), 1
    )
    cum = table_ref[:rows, :16]
    cum_t = table_ref[rows:, :]
    zero = jnp.zeros((rows, 128), jnp.bfloat16)
    normed = normalized(x_ref)
    for p in range(inner // 128):
        if p % (NB // 128) == 0:
            k = 128 * p // NB
            part = block_dot(normed, copies, buffer, k).astype(jnp.bfloat16)
            q_ref[:, NB * k : NB * (k + 1)] = part
        at = 128 * p % NB
        queries = part[:, at : at + 128]
        keys = kv_ref[:, 128 * p : 128 * (p + 1)]
        values = kv_ref[:, inner + 128 * p : inner + 128 * (p + 1)]
        weights = []
        for k in range(2):
            h = 2 * p + k
            own = jnp.where(low, queries, zero) if k == 0 else jnp.where(low, zero, queries)
            scores = lax.dot_general(
                own, keys, (((1,), (1,)), ((), ())), preferred_element_type=jnp.float32
            )
            gap = cum[:, h : h + 1] - cum_t[h : h + 1, :]
            decay = jnp.exp(jnp.where(causal, gap, 0.0))
            weights.append(jnp.where(causal, scores * decay, 0.0).astype(jnp.bfloat16))
        both = jnp.concatenate(
            [jnp.where(low, values, zero), jnp.where(low, zero, values)], axis=0
        )
        out_ref[:, 128 * p : 128 * (p + 1)] = jnp.dot(
            jnp.concatenate(weights, axis=1), both, preferred_element_type=jnp.float32
        )


def within(x, weights, kv, table):
    rows, width = x.shape
    inner = kv.shape[1] // 2
    share = width // 64
    blocks = [(share, [(side, 0, 0, NB)]) for side in range(2)]
    vmem = pl.BlockSpec(memory_space=pltpu.VMEM)
    return pl.pallas_call(
        functools.partial(within_kernel, blocks),
        in_specs=[vmem, pl.BlockSpec(memory_space=pl.ANY), vmem, vmem],
        out_specs=[vmem] * 2,
        out_shape=[
            jax.ShapeDtypeStruct((rows, inner), jnp.bfloat16),
            jax.ShapeDtypeStruct((rows, inner), jnp.float32),
        ],
        scratch_shapes=[
            pltpu.VMEM((len(blocks), 2, 32, share, NB), jnp.bfloat16),
            pltpu.SemaphoreType.DMA((len(blocks), 2)),
        ],
        compiler_params=pltpu.CompilerParams(vmem_limit_bytes=VMEM_KEPT),
        cost_estimate=pl.CostEstimate(
            flops=2 * rows * width * inner + 6 * rows * rows * inner,
            bytes_accessed=2 * width * inner + 16 * rows * inner,
            transcendentals=16 * rows * rows,
        ),
        name="within",
    )(x, weights, kv, table)


def carry_kernel(start_ref, state_ref, total_ref, out_ref):
    carried = jnp.zeros(state_ref.shape[1:], jnp.float32)
    count = state_ref.shape[0]
    start = start_ref[0]
    for i in range(count):
        c = start + i if i < count // 2 else i - start
        out_ref[c] = carried.astype(jnp.bfloat16)
        carried = total_ref[pl.ds(c, 1), :] * carried + state_ref[c].astype(jnp.float32)


def carry(states, totals, start):
    return pl.pallas_call(
        carry_kernel,
        in_specs=[pl.BlockSpec(memory_space=pltpu.SMEM)] + [pl.BlockSpec(memory_space=pltpu.VMEM)] * 2,
        out_specs=pl.BlockSpec(memory_space=pltpu.VMEM),
        out_shape=jax.ShapeDtypeStruct(states.shape, jnp.bfloat16),
        compiler_params=pltpu.CompilerParams(vmem_limit_bytes=4 * 2**20),
        cost_estimate=pl.CostEstimate(
            flops=2 * states.size, bytes_accessed=4 * states.size, transcendentals=0
        ),
        name="carry",
    )(start, states, totals)


def output_kernel(
    blocks, q_ref, carried_ref, table_ref, within_ref, x_ref, w_ref, out_ref, buffer, sems
):
    copies = share_copies(blocks, w_ref, buffer, sems)
    start_all(copies)
    rows, inner = within_ref.shape
    low = half_mask(rows, 128, 64)
    low64 = low[:64]
    zero = jnp.zeros((64, 128), jnp.bfloat16)
    grow = table_ref[:rows, 32:48]
    mixed = []
    for p in range(inner // 128):
        cols = slice(128 * p, 128 * (p + 1))
        state = carried_ref[64 * p : 64 * (p + 1), :]
        both = jnp.concatenate(
            [jnp.where(low64, state, zero), jnp.where(low64, zero, state)], axis=0
        )
        earlier = jnp.dot(q_ref[:, cols], both, preferred_element_type=jnp.float32)
        mixture = within_ref[:, cols] + earlier * by_head(low, grow, p)
        square = mixture * mixture
        first = jnp.sum(jnp.where(low, square, 0.0), axis=-1, keepdims=True)
        second = jnp.sum(jnp.where(low, 0.0, square), axis=-1, keepdims=True)
        scale = jnp.where(
            low, lax.rsqrt(first * (1.0 / 64.0) + EPS), lax.rsqrt(second * (1.0 / 64.0) + EPS)
        )
        mixed.append((mixture * scale).astype(jnp.bfloat16))
    mixed = jnp.concatenate(mixed, axis=1)
    for k in range(len(blocks)):
        cols = slice(NB * k, NB * (k + 1))
        acc = block_dot(mixed, copies, buffer, k)
        out_ref[:, cols] = (x_ref[:, cols].astype(jnp.float32) + acc).astype(jnp.bfloat16)


def output(q, carried, table, inside, x, weights):
    rows, width = x.shape
    inner = inside.shape[1]
    share = inner // 64
    first = 3 * (width // 64)
    blocks = [(share, [(n // 2, first + share * (n % 2), 0, NB)]) for n in range(4)]
    vmem = pl.BlockSpec(memory_space=pltpu.VMEM)
    return pl.pallas_call(
        functools.partial(output_kernel, blocks),
        in_specs=[vmem] * 5 + [pl.BlockSpec(memory_space=pl.ANY)],
        out_specs=vmem,
        out_shape=jax.ShapeDtypeStruct((rows, width), jnp.bfloat16),
        scratch_shapes=[
            pltpu.VMEM((len(blocks), 2, 32, share, NB), jnp.bfloat16),
            pltpu.SemaphoreType.DMA((len(blocks), 2)),
        ],
        compiler_params=pltpu.CompilerParams(vmem_limit_bytes=VMEM_KEPT),
        cost_estimate=pl.CostEstimate(
            flops=2 * rows * width * inner, bytes_accessed=2 * width * inner, transcendentals=0
        ),
        name="output",
    )(q, carried, table, inside, x, weights)


def paired(low, high, core):
    keep = jnp.where(core == 0, low, high)
    other = swap(jnp.where(core == 0, high, low), "core")
    return jnp.where(core == 0, keep, other), jnp.where(core == 0, other, keep)


def across(value, axes):
    flip = [(0, 3), (1, 2), (2, 1), (3, 0)] if len(axes) == 2 else [(0, 1), (1, 0)]
    return lax.ppermute(value, axes, flip)


def split_kernel(core_ref, qkv_ref, out_ref, keep_ref, give_ref):
    rows, depth = qkv_ref.shape[0], out_ref.shape[0]
    inner, wide = qkv_ref.shape[1] // 3, out_ref.shape[1] // 2
    core = core_ref[0]
    for side in range(2):
        for mine, goal in ((True, keep_ref), (False, give_ref)):

            @pl.when((core == side) == mine)
            def _(side=side, goal=goal):
                for i in range(3):
                    at = inner * i + NB * side
                    goal[rows * i : rows * (i + 1), :] = qkv_ref[:, at : at + NB]
                for i in range(2):
                    at, row = wide * side + NB * i, 3 * rows + depth * i
                    goal[row : row + depth, :] = out_ref[:, at : at + NB]


def split_halves(qkv, out, core):
    vmem = pl.BlockSpec(memory_space=pltpu.VMEM)
    half = jax.ShapeDtypeStruct(((qkv.size + out.size) // (2 * NB), NB), jnp.bfloat16)
    return pl.pallas_call(
        split_kernel,
        in_specs=[pl.BlockSpec(memory_space=pltpu.SMEM), vmem, vmem],
        out_specs=[vmem] * 2,
        out_shape=[half] * 2,
        compiler_params=pltpu.CompilerParams(vmem_limit_bytes=VMEM_KEPT),
        name="split",
    )(core.reshape(1).astype(jnp.int32), qkv, out)


def hand_over(value, hops):
    pairs = []
    for level, turn in hops:
        for core in range(2):
            for far in range(2):
                goal = far ^ core if turn else far
                pairs.append((level * 4 + core * 2 + far, (1 - level) * 4 + core * 2 + goal))
    return lax.ppermute(value, ("ylo", "core", "yhi"), pairs)


def shared_weights(qkv, out, core, level):
    keep, give = split_halves(qkv, out, core)
    other = swap(give, "core")
    first, second = jnp.where(core == 0, keep, other), jnp.where(core == 0, other, keep)
    stay = jnp.where(level == 0, first, second)
    leave = jnp.where(level == 0, second, first)
    far = across(stay, ("yhi",))
    come, come_far = across(leave, ("ylo",)), across(leave, ("ylo", "yhi"))
    place = lax.axis_index("yhi")
    gathered = []
    for layer in range(2):
        staying = level == layer
        pair = jnp.where(staying, stay, come), jnp.where(staying, far, come_far)
        own = jnp.concatenate(
            [jnp.where(place == 0, pair[0], pair[1]), jnp.where(place == 0, pair[1], pair[0])], axis=0
        )
        gathered.append(lax.all_gather(own, SPREAD, axis=0).reshape(-1, 2, own.shape[0], NB))
    return gathered


def decays(log_decay, core, level):
    first, second = paired(log_decay[0], log_decay[1], core)
    come = hand_over(jnp.where(level == 0, second, first), [(0, True), (1, False)])
    both = [jnp.where(level == 0, first, come), jnp.where(level == 0, come, second)]
    rows, heads = first.shape
    lower = jnp.tril(jnp.ones((rows, rows), jnp.float32))
    blocks = lax.axis_size(CTX)
    per_pair = blocks // (heads // 2)
    tables, rows_sent = [], []
    for d in both:
        cum = jnp.dot(lower, d, precision=lax.Precision.HIGHEST)
        ending = cum[-1:]
        total = jnp.exp(ending[0])
        lanes = jnp.repeat(total.reshape(heads // 2, 2), 64, axis=1)
        rows_sent.append(jnp.repeat(lanes, per_pair, axis=0))
        wide = jnp.concatenate([cum, jnp.exp(ending - cum), jnp.exp(cum)], axis=1)
        wide = jnp.pad(wide, ((0, 0), (0, rows - wide.shape[1])))
        tables.append(jnp.concatenate([wide, cum.T], axis=0))
    sent = jnp.stack(rows_sent, axis=1)
    received = lax.all_to_all(sent, CTX, 0, 0, tiled=True)
    return tables, [received[:, k, :] for k in range(2)]


def shards(tokens, qkv_weight, out_weight, log_decay):
    core = lax.axis_index("core")
    level = lax.axis_index("ylo")
    blocks = lax.axis_size(CTX)
    x = lax.dynamic_index_in_dim(tokens, core, 0, False)
    weights = shared_weights(qkv_weight[0], out_weight[0], core, level)
    tables, totals = decays(log_decay[0], core, level)
    x, totals, tables = lax.optimization_barrier((x, totals, tables))
    straight = jnp.zeros((1,), jnp.int32)
    turned = straight + core * (blocks // 2)
    kept = []
    for step in range(4):
        layer = step // 2
        table, w = tables[layer], weights[layer]
        keys_from = w
        if step > 0:
            _, source = lax.optimization_barrier((x, w))
            keys_from = fetch_keys(source, x.shape[1] // 64)
            x = hand_over(x, [(1 - step % 2, step < 3)])
            kept.append(x)
        kv, state = project_keys(x, keys_from, table)
        slices = lax.all_to_all(state.reshape(blocks, -1, 128), CTX, 0, 0, tiled=True)
        q, inside = within(x, w, kv, table)
        slices, inside = lax.optimization_barrier((slices, inside))
        mine = carry(slices, totals[layer], turned if step == 1 else straight)
        carried = lax.all_to_all(mine, CTX, 0, 0, tiled=True).reshape(state.shape)
        x = output(q, carried, table, inside, x, w)
        kept.append(x)
    first = jnp.where(level == 0, kept[0], kept[5])
    second = jnp.where(level == 0, kept[3], kept[6])
    other = swap(jnp.where(core == 0, second, first), "core")
    result = jnp.stack([jnp.where(core == 0, first, other), jnp.where(core == 0, other, second)])
    return result[None]


def solution(mesh):
    fine = Mesh(mesh.devices.reshape(2, 2, 2, 4, 8), ("ylo", "core") + CTX)
    section = ("ylo", "core")
    in_specs = (
        P(None, CTX, None),
        P(section, CTX, None),
        P(section, CTX, None),
        P(section, None, CTX, None),
    )
    return jax.shard_map(
        shards, mesh=fine, in_specs=in_specs, out_specs=P(section, None, CTX, None), check_vma=False
    )
```

```python
import functools

import jax
import jax.numpy as jnp
from jax import lax
from jax.experimental import pallas as pl
from jax.experimental.pallas import tpu as pltpu
from jax.sharding import Mesh, PartitionSpec as P

CTX = ("yhi", "x", "z")
SPREAD = ("x", "z", "core")
NB = 512
EPS = 1e-05
VMEM_KEPT = 50 * 2**20


def swap(value, axis):
    return lax.ppermute(value, axis, [(0, 1), (1, 0)])


def half_mask(rows, lanes, half):
    return lax.broadcasted_iota(jnp.int32, (rows, lanes), 1) < half


def by_head(low, table, p):
    return jnp.where(low, table[:, 2 * p : 2 * p + 1], table[:, 2 * p + 1 : 2 * p + 2])


def share_copies(blocks, w_ref, buffer, sems):
    copies = []
    stride = w_ref.shape[2] // 2
    for k, (rows, parts) in enumerate(blocks):
        block, at = [], 0
        for side, first, column, count in parts:
            for far in range(2):
                source = w_ref.at[:, side, pl.ds(far * stride + first, rows), pl.ds(column, count)]
                goal = buffer.at[k, far, :, :, pl.ds(at, count)]
                block.append(pltpu.make_async_copy(source, goal, sems.at[k, len(block)]))
            at += count
        copies.append(block)
    return copies


def start_all(copies):
    for block in copies:
        for copy in block:
            copy.start()


def block_dot(left, copies, buffer, k):
    for copy in copies[k]:
        copy.wait()
    return jnp.dot(left, buffer[k].reshape(left.shape[1], NB), preferred_element_type=jnp.float32)


def normalized(x_ref):
    x = x_ref[...].astype(jnp.float32)
    return (x * lax.rsqrt(jnp.mean(x * x, axis=-1, keepdims=True) + EPS)).astype(jnp.bfloat16)


def fetch_kernel(blocks, w_ref, out_ref, sems):
    copies = share_copies(blocks, w_ref, out_ref, sems)
    start_all(copies)
    for block in copies:
        for copy in block:
            copy.wait()


def key_blocks(share):
    half = NB // 2
    return [
        (share, [(side, share * part, half * i, half) for part in (1, 2)])
        for side in range(2)
        for i in range(2)
    ]


def fetch_keys(weights, share):
    return pl.pallas_call(
        functools.partial(fetch_kernel, key_blocks(share)),
        in_specs=[pl.BlockSpec(memory_space=pl.ANY)],
        out_specs=pl.BlockSpec(memory_space=pltpu.VMEM),
        out_shape=pltpu.VMEM((4, 2, 32, share, NB), jnp.bfloat16),
        scratch_shapes=[pltpu.SemaphoreType.DMA((4, 4))],
        compiler_params=pltpu.CompilerParams(vmem_limit_bytes=VMEM_KEPT),
        cost_estimate=pl.CostEstimate(flops=0, bytes_accessed=4 * 4 * 64 * share * NB, transcendentals=0),
        name="fetch",
    )(weights)


def fetched_keys_kernel(x_ref, buffer, table_ref, kv_ref, state_ref):
    keys_of([[]] * buffer.shape[0], x_ref, table_ref, kv_ref, state_ref, buffer)


def keys_kernel(blocks, x_ref, w_ref, table_ref, kv_ref, state_ref, buffer, sems):
    copies = share_copies(blocks, w_ref, buffer, sems)
    start_all(copies)
    keys_of(copies, x_ref, table_ref, kv_ref, state_ref, buffer)


def keys_of(copies, x_ref, table_ref, kv_ref, state_ref, buffer):
    rows = x_ref.shape[0]
    inner = kv_ref.shape[1] // 2
    normed = normalized(x_ref)
    low = half_mask(rows, 128, 64)
    scale = table_ref[:rows, 16:32]
    half = NB // 2
    for k in range(len(copies)):
        part = block_dot(normed, copies, buffer, k).astype(jnp.bfloat16)
        kv_ref[:, half * k : half * (k + 1)] = part[:, :half]
        kv_ref[:, inner + half * k : inner + half * (k + 1)] = part[:, half:]
        for c in range(half // 128):
            p = half * k // 128 + c
            keys = part[:, 128 * c : 128 * (c + 1)].astype(jnp.float32) * by_head(low, scale, p)
            outer = lax.dot_general(
                keys.astype(jnp.bfloat16),
                part[:, half + 128 * c : half + 128 * (c + 1)],
                (((0,), (0,)), ((), ())),
                preferred_element_type=jnp.float32,
            )
            state_ref[64 * p : 64 * (p + 1), :] = jnp.where(
                low[:64], outer[:64], outer[64:]
            ).astype(jnp.bfloat16)


def project_keys(x, weights, table):
    rows, width = x.shape
    inner = 1024
    share = width // 64
    blocks = key_blocks(share)
    vmem = pl.BlockSpec(memory_space=pltpu.VMEM)
    fetched = weights.ndim == 5
    scratch = [
        pltpu.VMEM((len(blocks), 2, 32, share, NB), jnp.bfloat16),
        pltpu.SemaphoreType.DMA((len(blocks), 4)),
    ]
    return pl.pallas_call(
        fetched_keys_kernel if fetched else functools.partial(keys_kernel, blocks),
        in_specs=[vmem, vmem if fetched else pl.BlockSpec(memory_space=pl.ANY), vmem],
        out_specs=[vmem] * 2,
        out_shape=[
            jax.ShapeDtypeStruct((rows, 2 * inner), jnp.bfloat16),
            jax.ShapeDtypeStruct((inner // 2, 128), jnp.bfloat16),
        ],
        scratch_shapes=[] if fetched else scratch,
        compiler_params=pltpu.CompilerParams(vmem_limit_bytes=16 * 2**20 if fetched else VMEM_KEPT),
        cost_estimate=pl.CostEstimate(
            flops=4 * rows * width * inner, bytes_accessed=4 * width * inner, transcendentals=0
        ),
        name="keys",
    )(x, weights, table)


def within_kernel(blocks, x_ref, w_ref, kv_ref, table_ref, q_ref, out_ref, buffer, sems):
    copies = share_copies(blocks, w_ref, buffer, sems)
    start_all(copies)
    rows = kv_ref.shape[0]
    inner = kv_ref.shape[1] // 2
    low = half_mask(rows, 128, 64)
    causal = lax.broadcasted_iota(jnp.int32, (rows, rows), 0) >= lax.broadcasted_iota(
        jnp.int32, (rows, rows), 1
    )
    cum = table_ref[:rows, :16]
    cum_t = table_ref[rows:, :]
    zero = jnp.zeros((rows, 128), jnp.bfloat16)
    normed = normalized(x_ref)
    for p in range(inner // 128):
        if p % (NB // 128) == 0:
            k = 128 * p // NB
            part = block_dot(normed, copies, buffer, k).astype(jnp.bfloat16)
            q_ref[:, NB * k : NB * (k + 1)] = part
        at = 128 * p % NB
        queries = part[:, at : at + 128]
        keys = kv_ref[:, 128 * p : 128 * (p + 1)]
        values = kv_ref[:, inner + 128 * p : inner + 128 * (p + 1)]
        weights = []
        for k in range(2):
            h = 2 * p + k
            own = jnp.where(low, queries, zero) if k == 0 else jnp.where(low, zero, queries)
            scores = lax.dot_general(
                own, keys, (((1,), (1,)), ((), ())), preferred_element_type=jnp.float32
            )
            gap = cum[:, h : h + 1] - cum_t[h : h + 1, :]
            decay = jnp.exp(jnp.where(causal, gap, 0.0))
            weights.append(jnp.where(causal, scores * decay, 0.0).astype(jnp.bfloat16))
        both = jnp.concatenate(
            [jnp.where(low, values, zero), jnp.where(low, zero, values)], axis=0
        )
        out_ref[:, 128 * p : 128 * (p + 1)] = jnp.dot(
            jnp.concatenate(weights, axis=1), both, preferred_element_type=jnp.float32
        )


def within(x, weights, kv, table):
    rows, width = x.shape
    inner = kv.shape[1] // 2
    share = width // 64
    blocks = [(share, [(side, 0, 0, NB)]) for side in range(2)]
    vmem = pl.BlockSpec(memory_space=pltpu.VMEM)
    return pl.pallas_call(
        functools.partial(within_kernel, blocks),
        in_specs=[vmem, pl.BlockSpec(memory_space=pl.ANY), vmem, vmem],
        out_specs=[vmem] * 2,
        out_shape=[
            jax.ShapeDtypeStruct((rows, inner), jnp.bfloat16),
            jax.ShapeDtypeStruct((rows, inner), jnp.float32),
        ],
        scratch_shapes=[
            pltpu.VMEM((len(blocks), 2, 32, share, NB), jnp.bfloat16),
            pltpu.SemaphoreType.DMA((len(blocks), 2)),
        ],
        compiler_params=pltpu.CompilerParams(vmem_limit_bytes=VMEM_KEPT),
        cost_estimate=pl.CostEstimate(
            flops=2 * rows * width * inner + 6 * rows * rows * inner,
            bytes_accessed=2 * width * inner + 16 * rows * inner,
            transcendentals=16 * rows * rows,
        ),
        name="within",
    )(x, weights, kv, table)


def carry_kernel(start_ref, state_ref, total_ref, out_ref):
    carried = jnp.zeros(state_ref.shape[1:], jnp.float32)
    count = state_ref.shape[0]
    start = start_ref[0]
    for i in range(count):
        c = start + i if i < count // 2 else i - start
        out_ref[c] = carried.astype(jnp.bfloat16)
        carried = total_ref[pl.ds(c, 1), :] * carried + state_ref[c].astype(jnp.float32)


def carry(states, totals, start):
    return pl.pallas_call(
        carry_kernel,
        in_specs=[pl.BlockSpec(memory_space=pltpu.SMEM)] + [pl.BlockSpec(memory_space=pltpu.VMEM)] * 2,
        out_specs=pl.BlockSpec(memory_space=pltpu.VMEM),
        out_shape=jax.ShapeDtypeStruct(states.shape, jnp.bfloat16),
        compiler_params=pltpu.CompilerParams(vmem_limit_bytes=4 * 2**20),
        cost_estimate=pl.CostEstimate(
            flops=2 * states.size, bytes_accessed=4 * states.size, transcendentals=0
        ),
        name="carry",
    )(start, states, totals)


def output_kernel(
    blocks, q_ref, carried_ref, table_ref, within_ref, x_ref, w_ref, out_ref, buffer, sems
):
    copies = share_copies(blocks, w_ref, buffer, sems)
    start_all(copies)
    rows, inner = within_ref.shape
    low = half_mask(rows, 128, 64)
    low64 = low[:64]
    zero = jnp.zeros((64, 128), jnp.bfloat16)
    grow = table_ref[:rows, 32:48]
    mixed = []
    for p in range(inner // 128):
        cols = slice(128 * p, 128 * (p + 1))
        state = carried_ref[64 * p : 64 * (p + 1), :]
        both = jnp.concatenate(
            [jnp.where(low64, state, zero), jnp.where(low64, zero, state)], axis=0
        )
        earlier = jnp.dot(q_ref[:, cols], both, preferred_element_type=jnp.float32)
        mixture = within_ref[:, cols] + earlier * by_head(low, grow, p)
        square = mixture * mixture
        first = jnp.sum(jnp.where(low, square, 0.0), axis=-1, keepdims=True)
        second = jnp.sum(jnp.where(low, 0.0, square), axis=-1, keepdims=True)
        scale = jnp.where(
            low, lax.rsqrt(first * (1.0 / 64.0) + EPS), lax.rsqrt(second * (1.0 / 64.0) + EPS)
        )
        mixed.append((mixture * scale).astype(jnp.bfloat16))
    mixed = jnp.concatenate(mixed, axis=1)
    for k in range(len(blocks)):
        cols = slice(NB * k, NB * (k + 1))
        acc = block_dot(mixed, copies, buffer, k)
        out_ref[:, cols] = (x_ref[:, cols].astype(jnp.float32) + acc).astype(jnp.bfloat16)


def output(q, carried, table, inside, x, weights):
    rows, width = x.shape
    inner = inside.shape[1]
    share = inner // 64
    first = 3 * (width // 64)
    blocks = [(share, [(n // 2, first + share * (n % 2), 0, NB)]) for n in range(4)]
    vmem = pl.BlockSpec(memory_space=pltpu.VMEM)
    return pl.pallas_call(
        functools.partial(output_kernel, blocks),
        in_specs=[vmem] * 5 + [pl.BlockSpec(memory_space=pl.ANY)],
        out_specs=vmem,
        out_shape=jax.ShapeDtypeStruct((rows, width), jnp.bfloat16),
        scratch_shapes=[
            pltpu.VMEM((len(blocks), 2, 32, share, NB), jnp.bfloat16),
            pltpu.SemaphoreType.DMA((len(blocks), 2)),
        ],
        compiler_params=pltpu.CompilerParams(vmem_limit_bytes=VMEM_KEPT),
        cost_estimate=pl.CostEstimate(
            flops=2 * rows * width * inner, bytes_accessed=2 * width * inner, transcendentals=0
        ),
        name="output",
    )(q, carried, table, inside, x, weights)


def paired(low, high, core):
    keep = jnp.where(core == 0, low, high)
    other = swap(jnp.where(core == 0, high, low), "core")
    return jnp.where(core == 0, keep, other), jnp.where(core == 0, other, keep)


def across(value, axes):
    flip = [(0, 3), (1, 2), (2, 1), (3, 0)] if len(axes) == 2 else [(0, 1), (1, 0)]
    return lax.ppermute(value, axes, flip)


def split_kernel(core_ref, qkv_ref, out_ref, keep_ref, give_ref):
    rows, depth = qkv_ref.shape[0], out_ref.shape[0]
    inner, wide = qkv_ref.shape[1] // 3, out_ref.shape[1] // 2
    core = core_ref[0]
    for side in range(2):
        for mine, goal in ((True, keep_ref), (False, give_ref)):

            @pl.when((core == side) == mine)
            def _(side=side, goal=goal):
                for i in range(3):
                    at = inner * i + NB * side
                    goal[rows * i : rows * (i + 1), :] = qkv_ref[:, at : at + NB]
                for i in range(2):
                    at, row = wide * side + NB * i, 3 * rows + depth * i
                    goal[row : row + depth, :] = out_ref[:, at : at + NB]


def split_halves(qkv, out, core):
    vmem = pl.BlockSpec(memory_space=pltpu.VMEM)
    half = jax.ShapeDtypeStruct(((qkv.size + out.size) // (2 * NB), NB), jnp.bfloat16)
    return pl.pallas_call(
        split_kernel,
        in_specs=[pl.BlockSpec(memory_space=pltpu.SMEM), vmem, vmem],
        out_specs=[vmem] * 2,
        out_shape=[half] * 2,
        compiler_params=pltpu.CompilerParams(vmem_limit_bytes=VMEM_KEPT),
        name="split",
    )(core.reshape(1).astype(jnp.int32), qkv, out)


def hand_over(value, hops):
    pairs = []
    for level, turn in hops:
        for core in range(2):
            for far in range(2):
                goal = far ^ core if turn else far
                pairs.append((level * 4 + core * 2 + far, (1 - level) * 4 + core * 2 + goal))
    return lax.ppermute(value, ("ylo", "core", "yhi"), pairs)


def shared_weights(qkv, out, core, level):
    keep, give = split_halves(qkv, out, core)
    other = swap(give, "core")
    first, second = jnp.where(core == 0, keep, other), jnp.where(core == 0, other, keep)
    stay = jnp.where(level == 0, first, second)
    leave = jnp.where(level == 0, second, first)
    far = across(stay, ("yhi",))
    come, come_far = across(leave, ("ylo",)), across(leave, ("ylo", "yhi"))
    place = lax.axis_index("yhi")
    gathered = []
    for layer in range(2):
        staying = level == layer
        pair = jnp.where(staying, stay, come), jnp.where(staying, far, come_far)
        own = jnp.concatenate(
            [jnp.where(place == 0, pair[0], pair[1]), jnp.where(place == 0, pair[1], pair[0])], axis=0
        )
        gathered.append(lax.all_gather(own, SPREAD, axis=0).reshape(-1, 2, own.shape[0], NB))
    return gathered


def decays(log_decay, core, level):
    first, second = paired(log_decay[0], log_decay[1], core)
    come = hand_over(jnp.where(level == 0, second, first), [(0, True), (1, False)])
    both = [jnp.where(level == 0, first, come), jnp.where(level == 0, come, second)]
    rows, heads = first.shape
    lower = jnp.tril(jnp.ones((rows, rows), jnp.float32))
    blocks = lax.axis_size(CTX)
    per_pair = blocks // (heads // 2)
    tables, rows_sent = [], []
    for d in both:
        cum = jnp.dot(lower, d, precision=lax.Precision.HIGHEST)
        ending = cum[-1:]
        total = jnp.exp(ending[0])
        lanes = jnp.repeat(total.reshape(heads // 2, 2), 64, axis=1)
        rows_sent.append(jnp.repeat(lanes, per_pair, axis=0))
        wide = jnp.concatenate([cum, jnp.exp(ending - cum), jnp.exp(cum)], axis=1)
        wide = jnp.pad(wide, ((0, 0), (0, rows - wide.shape[1])))
        tables.append(jnp.concatenate([wide, cum.T], axis=0))
    sent = jnp.stack(rows_sent, axis=1)
    received = lax.all_to_all(sent, CTX, 0, 0, tiled=True)
    return tables, [received[:, k, :] for k in range(2)]


def shards(tokens, qkv_weight, out_weight, log_decay):
    core = lax.axis_index("core")
    level = lax.axis_index("ylo")
    blocks = lax.axis_size(CTX)
    x = lax.dynamic_index_in_dim(tokens, core, 0, False)
    weights = shared_weights(qkv_weight[0], out_weight[0], core, level)
    tables, totals = decays(log_decay[0], core, level)
    x, totals, tables = lax.optimization_barrier((x, totals, tables))
    straight = jnp.zeros((1,), jnp.int32)
    turned = straight + core * (blocks // 2)
    kept = []
    for step in range(4):
        layer = step // 2
        table, w = tables[layer], weights[layer]
        keys_from = w
        if step > 0:
            _, source = lax.optimization_barrier((x, w))
            keys_from = fetch_keys(source, x.shape[1] // 64)
            x = hand_over(x, [(1 - step % 2, step < 3)])
            kept.append(x)
        kv, state = project_keys(x, keys_from, table)
        slices = lax.all_to_all(state.reshape(blocks, -1, 128), CTX, 0, 0, tiled=True)
        q, inside = within(x, w, kv, table)
        slices, inside = lax.optimization_barrier((slices, inside))
        mine = carry(slices, totals[layer], turned if step == 1 else straight)
        carried = lax.all_to_all(mine, CTX, 0, 0, tiled=True).reshape(state.shape)
        x = output(q, carried, table, inside, x, w)
        kept.append(x)
    first = jnp.where(level == 0, kept[0], kept[5])
    second = jnp.where(level == 0, kept[3], kept[6])
    early = lax.ppermute(first, "core", [(1, 0)])
    late = lax.ppermute(second, "core", [(0, 1)])
    other = jnp.where(core == 0, early, late)
    result = jnp.stack([jnp.where(core == 0, first, other), jnp.where(core == 0, other, second)])
    return result[None]


def solution(mesh):
    fine = Mesh(mesh.devices.reshape(2, 2, 2, 4, 8), ("ylo", "core") + CTX)
    section = ("ylo", "core")
    in_specs = (
        P(None, CTX, None),
        P(section, CTX, None),
        P(section, CTX, None),
        P(section, None, CTX, None),
    )
    return jax.shard_map(
        shards, mesh=fine, in_specs=in_specs, out_specs=P(section, None, CTX, None), check_vma=False
    )
```

```python
import functools

import jax
import jax.numpy as jnp
from jax import lax
from jax.experimental import pallas as pl
from jax.experimental.pallas import tpu as pltpu
from jax.sharding import Mesh, PartitionSpec as P

CTX = ("yhi", "x", "z")
SPREAD = ("x", "z", "core")
NB = 512
EPS = 1e-05
VMEM_KEPT = 50 * 2**20


def swap(value, axis):
    return lax.ppermute(value, axis, [(0, 1), (1, 0)])


def half_mask(rows, lanes, half):
    return lax.broadcasted_iota(jnp.int32, (rows, lanes), 1) < half


def by_head(low, table, p):
    return jnp.where(low, table[:, 2 * p : 2 * p + 1], table[:, 2 * p + 1 : 2 * p + 2])


def share_copies(blocks, w_ref, buffer, sems):
    copies = []
    stride = w_ref.shape[2] // 2
    for k, (rows, parts) in enumerate(blocks):
        block, at = [], 0
        for side, first, column, count in parts:
            for far in range(2):
                source = w_ref.at[:, side, pl.ds(far * stride + first, rows), pl.ds(column, count)]
                goal = buffer.at[k, far, :, :, pl.ds(at, count)]
                block.append(pltpu.make_async_copy(source, goal, sems.at[k, len(block)]))
            at += count
        copies.append(block)
    return copies


def start_all(copies):
    for block in copies:
        for copy in block:
            copy.start()


def block_dot(left, copies, buffer, k):
    for copy in copies[k]:
        copy.wait()
    return jnp.dot(left, buffer[k].reshape(left.shape[1], NB), preferred_element_type=jnp.float32)


def normalized(x_ref):
    x = x_ref[...].astype(jnp.float32)
    return (x * lax.rsqrt(jnp.mean(x * x, axis=-1, keepdims=True) + EPS)).astype(jnp.bfloat16)


def fetch_kernel(blocks, w_ref, out_ref, sems):
    copies = share_copies(blocks, w_ref, out_ref, sems)
    start_all(copies)
    for block in copies:
        for copy in block:
            copy.wait()


def key_blocks(share):
    half = NB // 2
    return [
        (share, [(side, share * part, half * i, half) for part in (1, 2)])
        for side in range(2)
        for i in range(2)
    ]


def fetch_keys(weights, share):
    return pl.pallas_call(
        functools.partial(fetch_kernel, key_blocks(share)),
        in_specs=[pl.BlockSpec(memory_space=pl.ANY)],
        out_specs=pl.BlockSpec(memory_space=pltpu.VMEM),
        out_shape=pltpu.VMEM((4, 2, 32, share, NB), jnp.bfloat16),
        scratch_shapes=[pltpu.SemaphoreType.DMA((4, 4))],
        compiler_params=pltpu.CompilerParams(vmem_limit_bytes=VMEM_KEPT),
        cost_estimate=pl.CostEstimate(flops=0, bytes_accessed=4 * 4 * 64 * share * NB, transcendentals=0),
        name="fetch",
    )(weights)


def fetched_keys_kernel(x_ref, buffer, table_ref, kv_ref, state_ref):
    keys_of([[]] * buffer.shape[0], x_ref, table_ref, kv_ref, state_ref, buffer)


def keys_kernel(blocks, x_ref, w_ref, table_ref, kv_ref, state_ref, buffer, sems):
    copies = share_copies(blocks, w_ref, buffer, sems)
    start_all(copies)
    keys_of(copies, x_ref, table_ref, kv_ref, state_ref, buffer)


def keys_of(copies, x_ref, table_ref, kv_ref, state_ref, buffer):
    rows = x_ref.shape[0]
    inner = kv_ref.shape[1] // 2
    normed = normalized(x_ref)
    low = half_mask(rows, 128, 64)
    scale = table_ref[:rows, 16:32]
    half = NB // 2
    for k in range(len(copies)):
        part = block_dot(normed, copies, buffer, k).astype(jnp.bfloat16)
        kv_ref[:, half * k : half * (k + 1)] = part[:, :half]
        kv_ref[:, inner + half * k : inner + half * (k + 1)] = part[:, half:]
        for c in range(half // 128):
            p = half * k // 128 + c
            keys = part[:, 128 * c : 128 * (c + 1)].astype(jnp.float32) * by_head(low, scale, p)
            outer = lax.dot_general(
                keys.astype(jnp.bfloat16),
                part[:, half + 128 * c : half + 128 * (c + 1)],
                (((0,), (0,)), ((), ())),
                preferred_element_type=jnp.float32,
            )
            state_ref[64 * p : 64 * (p + 1), :] = jnp.where(
                low[:64], outer[:64], outer[64:]
            ).astype(jnp.bfloat16)


def project_keys(x, weights, table):
    rows, width = x.shape
    inner = 1024
    share = width // 64
    blocks = key_blocks(share)
    vmem = pl.BlockSpec(memory_space=pltpu.VMEM)
    fetched = weights.ndim == 5
    scratch = [
        pltpu.VMEM((len(blocks), 2, 32, share, NB), jnp.bfloat16),
        pltpu.SemaphoreType.DMA((len(blocks), 4)),
    ]
    return pl.pallas_call(
        fetched_keys_kernel if fetched else functools.partial(keys_kernel, blocks),
        in_specs=[vmem, vmem if fetched else pl.BlockSpec(memory_space=pl.ANY), vmem],
        out_specs=[vmem] * 2,
        out_shape=[
            jax.ShapeDtypeStruct((rows, 2 * inner), jnp.bfloat16),
            jax.ShapeDtypeStruct((inner // 2, 128), jnp.bfloat16),
        ],
        scratch_shapes=[] if fetched else scratch,
        compiler_params=pltpu.CompilerParams(vmem_limit_bytes=16 * 2**20 if fetched else VMEM_KEPT),
        cost_estimate=pl.CostEstimate(
            flops=4 * rows * width * inner, bytes_accessed=4 * width * inner, transcendentals=0
        ),
        name="keys",
    )(x, weights, table)


def within_kernel(blocks, x_ref, w_ref, kv_ref, table_ref, q_ref, out_ref, buffer, sems):
    copies = share_copies(blocks, w_ref, buffer, sems)
    start_all(copies)
    rows = kv_ref.shape[0]
    inner = kv_ref.shape[1] // 2
    low = half_mask(rows, 128, 64)
    causal = lax.broadcasted_iota(jnp.int32, (rows, rows), 0) >= lax.broadcasted_iota(
        jnp.int32, (rows, rows), 1
    )
    cum = table_ref[:rows, :16]
    cum_t = table_ref[rows:, :]
    zero = jnp.zeros((rows, 128), jnp.bfloat16)
    normed = normalized(x_ref)
    for p in range(inner // 128):
        if p % (NB // 128) == 0:
            k = 128 * p // NB
            part = block_dot(normed, copies, buffer, k).astype(jnp.bfloat16)
            q_ref[:, NB * k : NB * (k + 1)] = part
        at = 128 * p % NB
        queries = part[:, at : at + 128]
        keys = kv_ref[:, 128 * p : 128 * (p + 1)]
        values = kv_ref[:, inner + 128 * p : inner + 128 * (p + 1)]
        weights = []
        for k in range(2):
            h = 2 * p + k
            own = jnp.where(low, queries, zero) if k == 0 else jnp.where(low, zero, queries)
            scores = lax.dot_general(
                own, keys, (((1,), (1,)), ((), ())), preferred_element_type=jnp.float32
            )
            gap = cum[:, h : h + 1] - cum_t[h : h + 1, :]
            decay = jnp.exp(jnp.where(causal, gap, 0.0))
            weights.append(jnp.where(causal, scores * decay, 0.0).astype(jnp.bfloat16))
        both = jnp.concatenate(
            [jnp.where(low, values, zero), jnp.where(low, zero, values)], axis=0
        )
        out_ref[:, 128 * p : 128 * (p + 1)] = jnp.dot(
            jnp.concatenate(weights, axis=1), both, preferred_element_type=jnp.float32
        )


def within(x, weights, kv, table):
    rows, width = x.shape
    inner = kv.shape[1] // 2
    share = width // 64
    blocks = [(share, [(side, 0, 0, NB)]) for side in range(2)]
    vmem = pl.BlockSpec(memory_space=pltpu.VMEM)
    return pl.pallas_call(
        functools.partial(within_kernel, blocks),
        in_specs=[vmem, pl.BlockSpec(memory_space=pl.ANY), vmem, vmem],
        out_specs=[vmem] * 2,
        out_shape=[
            jax.ShapeDtypeStruct((rows, inner), jnp.bfloat16),
            jax.ShapeDtypeStruct((rows, inner), jnp.float32),
        ],
        scratch_shapes=[
            pltpu.VMEM((len(blocks), 2, 32, share, NB), jnp.bfloat16),
            pltpu.SemaphoreType.DMA((len(blocks), 2)),
        ],
        compiler_params=pltpu.CompilerParams(vmem_limit_bytes=VMEM_KEPT),
        cost_estimate=pl.CostEstimate(
            flops=2 * rows * width * inner + 6 * rows * rows * inner,
            bytes_accessed=2 * width * inner + 16 * rows * inner,
            transcendentals=16 * rows * rows,
        ),
        name="within",
    )(x, weights, kv, table)


def carry_kernel(start_ref, state_ref, total_ref, out_ref):
    carried = jnp.zeros(state_ref.shape[1:], jnp.float32)
    count = state_ref.shape[0]
    start = start_ref[0]
    for i in range(count):
        c = start + i if i < count // 2 else i - start
        out_ref[c] = carried.astype(jnp.bfloat16)
        carried = total_ref[pl.ds(c, 1), :] * carried + state_ref[c].astype(jnp.float32)


def carry(states, totals, start):
    return pl.pallas_call(
        carry_kernel,
        in_specs=[pl.BlockSpec(memory_space=pltpu.SMEM)] + [pl.BlockSpec(memory_space=pltpu.VMEM)] * 2,
        out_specs=pl.BlockSpec(memory_space=pltpu.VMEM),
        out_shape=jax.ShapeDtypeStruct(states.shape, jnp.bfloat16),
        compiler_params=pltpu.CompilerParams(vmem_limit_bytes=4 * 2**20),
        cost_estimate=pl.CostEstimate(
            flops=2 * states.size, bytes_accessed=4 * states.size, transcendentals=0
        ),
        name="carry",
    )(start, states, totals)


def output_kernel(
    blocks, q_ref, carried_ref, table_ref, within_ref, x_ref, w_ref, out_ref, buffer, sems
):
    copies = share_copies(blocks, w_ref, buffer, sems)
    start_all(copies)
    rows, inner = within_ref.shape
    low = half_mask(rows, 128, 64)
    low64 = low[:64]
    zero = jnp.zeros((64, 128), jnp.bfloat16)
    grow = table_ref[:rows, 32:48]
    mixed = []
    for p in range(inner // 128):
        cols = slice(128 * p, 128 * (p + 1))
        state = carried_ref[64 * p : 64 * (p + 1), :]
        both = jnp.concatenate(
            [jnp.where(low64, state, zero), jnp.where(low64, zero, state)], axis=0
        )
        earlier = jnp.dot(q_ref[:, cols], both, preferred_element_type=jnp.float32)
        mixture = within_ref[:, cols] + earlier * by_head(low, grow, p)
        square = mixture * mixture
        first = jnp.sum(jnp.where(low, square, 0.0), axis=-1, keepdims=True)
        second = jnp.sum(jnp.where(low, 0.0, square), axis=-1, keepdims=True)
        scale = jnp.where(
            low, lax.rsqrt(first * (1.0 / 64.0) + EPS), lax.rsqrt(second * (1.0 / 64.0) + EPS)
        )
        mixed.append((mixture * scale).astype(jnp.bfloat16))
    mixed = jnp.concatenate(mixed, axis=1)
    for k in range(len(blocks)):
        cols = slice(NB * k, NB * (k + 1))
        acc = block_dot(mixed, copies, buffer, k)
        out_ref[:, cols] = (x_ref[:, cols].astype(jnp.float32) + acc).astype(jnp.bfloat16)


def output(q, carried, table, inside, x, weights):
    rows, width = x.shape
    inner = inside.shape[1]
    share = inner // 64
    first = 3 * (width // 64)
    blocks = [(share, [(n // 2, first + share * (n % 2), 0, NB)]) for n in range(4)]
    vmem = pl.BlockSpec(memory_space=pltpu.VMEM)
    return pl.pallas_call(
        functools.partial(output_kernel, blocks),
        in_specs=[vmem] * 5 + [pl.BlockSpec(memory_space=pl.ANY)],
        out_specs=vmem,
        out_shape=jax.ShapeDtypeStruct((rows, width), jnp.bfloat16),
        scratch_shapes=[
            pltpu.VMEM((len(blocks), 2, 32, share, NB), jnp.bfloat16),
            pltpu.SemaphoreType.DMA((len(blocks), 2)),
        ],
        compiler_params=pltpu.CompilerParams(vmem_limit_bytes=VMEM_KEPT),
        cost_estimate=pl.CostEstimate(
            flops=2 * rows * width * inner, bytes_accessed=2 * width * inner, transcendentals=0
        ),
        name="output",
    )(q, carried, table, inside, x, weights)


def paired(low, high, core):
    keep = jnp.where(core == 0, low, high)
    other = swap(jnp.where(core == 0, high, low), "core")
    return jnp.where(core == 0, keep, other), jnp.where(core == 0, other, keep)


def across(value, axes):
    flip = [(0, 3), (1, 2), (2, 1), (3, 0)] if len(axes) == 2 else [(0, 1), (1, 0)]
    return lax.ppermute(value, axes, flip)


def split_kernel(core_ref, qkv_ref, out_ref, keep_ref, give_ref):
    rows, depth = qkv_ref.shape[0], out_ref.shape[0]
    inner, wide = qkv_ref.shape[1] // 3, out_ref.shape[1] // 2
    core = core_ref[0]
    for side in range(2):
        for mine, goal in ((True, keep_ref), (False, give_ref)):

            @pl.when((core == side) == mine)
            def _(side=side, goal=goal):
                for i in range(3):
                    at = inner * i + NB * side
                    goal[rows * i : rows * (i + 1), :] = qkv_ref[:, at : at + NB]
                for i in range(2):
                    at, row = wide * side + NB * i, 3 * rows + depth * i
                    goal[row : row + depth, :] = out_ref[:, at : at + NB]


def split_halves(qkv, out, core):
    vmem = pl.BlockSpec(memory_space=pltpu.VMEM)
    half = jax.ShapeDtypeStruct(((qkv.size + out.size) // (2 * NB), NB), jnp.bfloat16)
    return pl.pallas_call(
        split_kernel,
        in_specs=[pl.BlockSpec(memory_space=pltpu.SMEM), vmem, vmem],
        out_specs=[vmem] * 2,
        out_shape=[half] * 2,
        compiler_params=pltpu.CompilerParams(vmem_limit_bytes=VMEM_KEPT),
        name="split",
    )(core.reshape(1).astype(jnp.int32), qkv, out)


def hand_over(value, hops):
    pairs = []
    for level, turn in hops:
        for core in range(2):
            for far in range(2):
                goal = far ^ (1 - core) if turn else far
                pairs.append((level * 4 + core * 2 + far, (1 - level) * 4 + core * 2 + goal))
    return lax.ppermute(value, ("ylo", "core", "yhi"), pairs)


def shared_weights(qkv, out, core, level):
    keep, give = split_halves(qkv, out, core)
    other = swap(give, "core")
    first, second = jnp.where(core == 0, keep, other), jnp.where(core == 0, other, keep)
    stay = jnp.where(level == 0, first, second)
    leave = jnp.where(level == 0, second, first)
    far = across(stay, ("yhi",))
    come, come_far = across(leave, ("ylo",)), across(leave, ("ylo", "yhi"))
    place = lax.axis_index("yhi")
    gathered = []
    for layer in range(2):
        staying = level == layer
        pair = jnp.where(staying, stay, come), jnp.where(staying, far, come_far)
        own = jnp.concatenate(
            [jnp.where(place == 0, pair[0], pair[1]), jnp.where(place == 0, pair[1], pair[0])], axis=0
        )
        gathered.append(lax.all_gather(own, SPREAD, axis=0).reshape(-1, 2, own.shape[0], NB))
    return gathered


def decays(log_decay, core, level):
    first, second = paired(log_decay[0], log_decay[1], core)
    come = hand_over(jnp.where(level == 0, second, first), [(0, True), (1, False)])
    both = [jnp.where(level == 0, first, come), jnp.where(level == 0, come, second)]
    rows, heads = first.shape
    lower = jnp.tril(jnp.ones((rows, rows), jnp.float32))
    blocks = lax.axis_size(CTX)
    per_pair = blocks // (heads // 2)
    tables, rows_sent = [], []
    for d in both:
        cum = jnp.dot(lower, d, precision=lax.Precision.HIGHEST)
        ending = cum[-1:]
        total = jnp.exp(ending[0])
        lanes = jnp.repeat(total.reshape(heads // 2, 2), 64, axis=1)
        rows_sent.append(jnp.repeat(lanes, per_pair, axis=0))
        wide = jnp.concatenate([cum, jnp.exp(ending - cum), jnp.exp(cum)], axis=1)
        wide = jnp.pad(wide, ((0, 0), (0, rows - wide.shape[1])))
        tables.append(jnp.concatenate([wide, cum.T], axis=0))
    sent = jnp.stack(rows_sent, axis=1)
    received = lax.all_to_all(sent, CTX, 0, 0, tiled=True)
    return tables, [received[:, k, :] for k in range(2)]


def shards(tokens, qkv_weight, out_weight, log_decay):
    core = lax.axis_index("core")
    level = lax.axis_index("ylo")
    blocks = lax.axis_size(CTX)
    x = lax.dynamic_index_in_dim(tokens, core, 0, False)
    weights = shared_weights(qkv_weight[0], out_weight[0], core, level)
    tables, totals = decays(log_decay[0], core, level)
    x, totals, tables = lax.optimization_barrier((x, totals, tables))
    straight = jnp.zeros((1,), jnp.int32)
    turned = straight + (1 - core) * (blocks // 2)
    kept = []
    for step in range(4):
        layer = step // 2
        table, w = tables[layer], weights[layer]
        keys_from = w
        if step > 0:
            _, source = lax.optimization_barrier((x, w))
            keys_from = fetch_keys(source, x.shape[1] // 64)
            x = hand_over(x, [(1 - step % 2, step < 3)])
            kept.append(x)
        kv, state = project_keys(x, keys_from, table)
        slices = lax.all_to_all(state.reshape(blocks, -1, 128), CTX, 0, 0, tiled=True)
        q, inside = within(x, w, kv, table)
        slices, inside = lax.optimization_barrier((slices, inside))
        mine = carry(slices, totals[layer], turned if step == 1 else straight)
        carried = lax.all_to_all(mine, CTX, 0, 0, tiled=True).reshape(state.shape)
        x = output(q, carried, table, inside, x, w)
        kept.append(x)
    first = jnp.where(level == 0, kept[0], kept[5])
    second = jnp.where(level == 0, kept[3], kept[6])
    other = swap(jnp.where(core == 0, second, first), "core")
    result = jnp.stack([jnp.where(core == 0, first, other), jnp.where(core == 0, other, second)])
    return result[None]


def solution(mesh):
    fine = Mesh(mesh.devices.reshape(2, 2, 2, 4, 8), ("ylo", "core") + CTX)
    section = ("ylo", "core")
    in_specs = (
        P(None, CTX, None),
        P(section, CTX, None),
        P(section, CTX, None),
        P(section, None, CTX, None),
    )
    return jax.shard_map(
        shards, mesh=fine, in_specs=in_specs, out_specs=P(section, None, CTX, None), check_vma=False
    )
```
